256 devices in a mesh: row: 32 (over x_hi, z, core), col: 8 (over y, x_lo).
Axes of the slice: x: 4 (x_hi: 2, x_lo: 2; x = x_hi * 2 + x_lo), y: 4, z: 8, core: 2. Of those that a mesh axis runs over, the one named last changes fastest.
Arguments:
- features: bfloat16 [8, 8192, 128], P('col', 'row'), may hold values from -6 to 6
- tiles: bfloat16 [32, 8, 256, 128, 128], P('row', 'col'), may hold values from -0.15625 to 0.15625
- tile_rows: int32 [32, 8, 256], P('row', 'col'), may hold values from 0 to 15
- tile_cols: int32 [32, 8, 256], P('row', 'col'), may hold values from 0 to 63
- tile_count: int32 [32, 8], P('row', 'col'), may hold values from 32 to 256, as said below
- weight: bfloat16 [128, 128], replicated, may hold values from -0.5 to 0.5
- grad_out: bfloat16 [32, 2048, 128], P('row', 'col'), may hold values from -6 to 6
Outputs:
- layer_out: bfloat16 [32, 2048, 128], P('row', 'col')
- grad_features: bfloat16 [8, 8192, 128], P('col', 'row')
- grad_weight: float32 [128, 128], replicated
The draws below stay inside these ranges and needn't reach their ends.
Inputs may be any that keep to these rules, and one draw needn't show every extreme that they name: tile_count[r, c] slots of device (r, c), the first ones of its list, are live; the rest are ignored. Some device holds 256 live tiles in every draw.
All inputs are finite; a program needn't handle non-finite values.
Results may differ from the reference program's by a relative error of at most 0.022.
Values may be sent and summed in bfloat16 or wider, within the bound.
A program may use at most 128 MiB of HBM per device.

```python
import math
import jax
import jax.numpy as jnp
from jax import lax

F = 128
TB = 128
NB_DEV = 2
TILE_DEV = 256
NODES = 65536
ROW_NODES = 2048
COL_NODES = 8192
N_ROW = 32
N_COL = 8


def draw_tile_count(key, part):
    key = jax.random.fold_in(key, 5)
    shift_key, pick_key = jax.random.split(key)
    shifts = jax.random.randint(shift_key, (N_ROW * N_COL,), 0, 4)
    counts = TILE_DEV // jnp.power(2, shifts).astype(jnp.int32)
    chosen = jax.random.randint(pick_key, (), 0, N_ROW * N_COL)
    positions = jnp.arange(N_ROW * N_COL)
    counts = jnp.where(positions == chosen, TILE_DEV, counts)
    return counts.reshape(N_ROW, N_COL).astype(jnp.int32)


def touch_ends(array, rng, least, largest):
    place = [jax.random.randint(jax.random.fold_in(rng, axis), (), 0, length) for axis, length in enumerate(array.shape)]
    longest = array.shape.index(max(array.shape))
    neighbour = place[:longest] + [(place[longest] + 1) % array.shape[longest]] + place[longest + 1:]
    return array.at[tuple(place)].set(least).at[tuple(neighbour)].set(largest)


def steps_of(stream_key, shape, pieces, low, top_value):
    loudness = 1.0
    for axis_at, parts in pieces:
        draws = jax.random.uniform(jax.random.fold_in(jax.random.fold_in(stream_key, 6), axis_at), (parts,), jnp.float32, low / len(pieces), top_value / len(pieces))
        loudness = loudness * jnp.repeat(jnp.exp(draws), shape[axis_at] // parts).reshape((-1,) + (1,) * (len(shape) - 1 - axis_at))
    return loudness


def noise(own_key, extent, deviation, limit, shards=(), dtype=jnp.bfloat16):
    drawn = deviation * jax.random.normal(own_key, extent, jnp.float32)
    if shards:
        drawn = drawn * steps_of(own_key, extent, shards, -0.22, 0.18)
    return jnp.clip(drawn, -limit, limit).astype(dtype)


def setup_inputs(seed: int = 0) -> dict:
    seeds = jax.random.split(jax.random.key(seed), 8)
    return {
        "features": noise(seeds[0], (N_COL, COL_NODES, F), 1.0, 6.0, ((0, 8), (1, 32))),
        "tiles": noise(seeds[1], (N_ROW, N_COL, TILE_DEV, TB, TB), ((2 * NB_DEV / (TB * TILE_DEV)) ** 0.5), 0.15625, ((0, 32), (1, 8))),
        "tile_rows": touch_ends(jax.random.randint(seeds[2], (N_ROW, N_COL, TILE_DEV), 0, NB_DEV * N_COL), jax.random.fold_in(seeds[2], 1), 0, (NB_DEV * N_COL) - 1).astype(jnp.int32),
        "tile_cols": touch_ends(jax.random.randint(seeds[3], (N_ROW, N_COL, TILE_DEV), 0, NB_DEV * N_ROW), jax.random.fold_in(seeds[3], 1), 0, (NB_DEV * N_ROW) - 1).astype(jnp.int32),
        "tile_count": draw_tile_count(jax.random.fold_in(seeds[7], 71), 0),
        "weight": noise(seeds[5], (F, F), F ** -0.5, 0.5),
        "grad_out": noise(seeds[6], (N_ROW, ROW_NODES, F), 1.0, 6.0, ((0, 32), (1, 8))),
    }


def reference(features, tiles, tile_rows, tile_cols, tile_count, weight, grad_out):
    col_blocks = NB_DEV * N_ROW
    row_blocks = NB_DEV * N_COL
    feature_blocks = features.reshape(N_COL, col_blocks, TB, F).astype(jnp.float32)
    live_mask = (jnp.arange(TILE_DEV)[None, None, :] < tile_count[:, :, None]).astype(jnp.float32)
    group_index = jnp.arange(N_COL)[:, None]

    def forward_group(inputs):
        tile_group, row_index, col_index, live_group = inputs
        picked = feature_blocks[group_index, col_index]
        product = jnp.einsum('csij,csjf->csif', tile_group.astype(jnp.float32), picked)
        product = product * live_group[:, :, None, None]
        summed = jax.ops.segment_sum(product.reshape(-1, TB, F), row_index.reshape(-1), num_segments=row_blocks)
        return summed.reshape(row_blocks * TB, F).astype(jnp.bfloat16)
    aggregated = lax.map(forward_group, (tiles, tile_rows, tile_cols, live_mask))
    agg_flat = aggregated.reshape(-1, F)
    layer_out = jnp.dot(agg_flat, weight, preferred_element_type=jnp.float32).astype(jnp.bfloat16)
    layer_out = layer_out.reshape(N_ROW, -1, F)
    grad_flat = grad_out.reshape(-1, F)
    grad_agg = jnp.dot(grad_flat, weight.T, preferred_element_type=jnp.float32).astype(jnp.bfloat16)
    grad_blocks = grad_agg.reshape(N_ROW, row_blocks, TB, F)
    grad_weight = jnp.dot(agg_flat.T, grad_flat, preferred_element_type=jnp.float32) / math.sqrt(NODES)

    def segment_cols(product_group, col_group):
        return jax.ops.segment_sum(product_group, col_group, num_segments=col_blocks)

    def backward_group(carry, inputs):
        tile_group, row_index, col_index, live_group, grad_group = inputs
        picked = grad_group.astype(jnp.float32)[row_index]
        product = jnp.einsum('csij,csif->csjf', tile_group.astype(jnp.float32), picked)
        product = product * live_group[:, :, None, None]
        return (carry + jax.vmap(segment_cols)(product, col_index), None)
    start = jnp.zeros((N_COL, col_blocks, TB, F), jnp.float32)
    total, _ = lax.scan(backward_group, start, (tiles, tile_rows, tile_cols, live_mask, grad_blocks))
    grad_features = total.reshape(N_COL, -1, F).astype(jnp.bfloat16)
    return (layer_out, grad_features, grad_weight)
```

```python
import math

import jax
import jax.numpy as jnp
from jax import lax
from jax.experimental import pallas as pl
from jax.experimental.pallas import tpu as pltpu
from jax.sharding import PartitionSpec as P

TB = 128
F = 128
SLOTS = 256
ROW_BLOCKS = 16
COL_BLOCKS = 64
NZ = 8
NCOL = 8
UNROLL = 32
STEPS = SLOTS // UNROLL
EMPTY = SLOTS
B_ORDER, B_LAST = 0, 256
F_ORDER, F_LAST = 320, 576
PLAN = 592
PIECES = ((0, 1), (1, 2), (3, 2), (5, 2), (7, 1))


def tile_plan(rows, cols, count):
    slot = jnp.arange(SLOTS, dtype=jnp.int32)
    live = slot < count
    key = jnp.stack([jnp.where(live, cols, 64), jnp.where(live, rows, 64)])
    other = jnp.stack([rows, cols])
    value = key * 65536 + slot[None, :] * 256 + other
    place = jnp.sum(value[:, None, :] < value[:, :, None], axis=2, dtype=jnp.int32)
    hit = place[:, None, :] == slot[None, :, None]
    order = jnp.sum(jnp.where(hit, value[:, None, :], 0), axis=2, dtype=jnp.int32)
    block = jnp.arange(COL_BLOCKS, dtype=jnp.int32)
    upto = jnp.sum(key[:, None, :] <= block[None, :, None], axis=2, dtype=jnp.int32)
    some = jnp.any(key[:, None, :] == block[None, :, None], axis=2)
    last = jnp.where(some, upto - 1, EMPTY)
    return jnp.concatenate([order[0], last[0], order[1], last[1, :ROW_BLOCKS]])


def remote(src, dst, send, recv, device):
    return pltpu.make_async_remote_copy(
        src_ref=src, dst_ref=dst, send_sem=send, recv_sem=recv,
        device_id=device, device_id_type=pl.DeviceIdType.MESH,
    )


def kernel(
    plan, feat, gout, w, tiles_hbm, lay_ref, gf_ref, gw_ref,
    tv, fbuf, gbuf, gagg, runs, part, peer, ring_out, ring_in, x_out, x_in,
    agg, agg_in, wt, red1, red2, red3, red4,
    tile_sem, col_s, col_r, agz_s, agz_r, agx, agp_s, agp_r,
    rp_s, rp_r, rz_s, rz_r, rx, cr_s, cr_r,
    a1_s, a1_r, a2_s, a2_r, a3_s, a3_r, a4_s, a4_r,
):
    r = lax.axis_index("row")
    c = lax.axis_index("col")
    core = lax.rem(r, 2)
    z = lax.rem(r // 2, NZ)
    xh = r // (2 * NZ)

    def rid(a, b, k):
        return (a * NZ + b) * 2 + k

    def zrel(o):
        return lax.rem(z + (o % NZ), NZ)

    def crel(o):
        return lax.rem(c + (o % NCOL), NCOL)

    up = (rid(xh, zrel(1), core), c)
    down = (rid(xh, zrel(-1), core), c)
    partner = (rid(xh, z, 1 - core), c)
    opposite = (rid(1 - xh, z, core), c)
    diagonal = (rid(1 - xh, z, 1 - core), c)
    zpeer = [None] + [(rid(xh, zrel(i), core), c) for i in range(1, NZ)]
    cpeer = [None] + [(r, crel(i)) for i in range(1, NCOL)]

    tile_copies = [
        pltpu.make_async_copy(
            tiles_hbm.at[pl.ds(64 * i, 64)], tv.at[pl.ds(64 * i, 64)], tile_sem.at[i]
        )
        for i in range(4)
    ]
    for copy in tile_copies:
        copy.start()
    barrier = pltpu.get_barrier_semaphore()
    everyone = zpeer[1:] + cpeer[1:] + [partner, opposite, diagonal]
    for device in everyone:
        pl.semaphore_signal(
            barrier, inc=1, device_id=device, device_id_type=pl.DeviceIdType.MESH
        )
    fbuf[pl.ds(2 * r, 2)] = feat[...]
    gbuf[pl.ds(2 * c, 2)] = gout[...]
    runs[EMPTY] = jnp.zeros((TB, F), jnp.float32)
    pl.semaphore_wait(barrier, len(everyone))

    def col_copy(i, owner):
        here = gbuf.at[pl.ds(2 * owner, 2)]
        return remote(here, here, col_s.at[i - 1], col_r.at[i - 1], cpeer[i])

    for i in range(1, NCOL):
        col_copy(i, c).start()

    def shard(st, o):
        return 2 * rid(xh if st == 0 else 1 - xh, zrel(o), core)

    def z_copy(st, way, step, first, size):
        here = fbuf.at[pl.ds(first, size)]
        return remote(
            here, here, agz_s.at[st, way, step], agz_r.at[st, way, step], up if way == 0 else down
        )

    def p_copy(st, o, mine=True):
        k = core if mine else 1 - core
        first = 2 * rid(xh if st == 0 else 1 - xh, zrel(o), k)
        here = fbuf.at[pl.ds(first, 2)]
        return remote(here, here, agp_s.at[st, o % NZ], agp_r.at[st, o % NZ], partner)

    def x_copy(first):
        here = fbuf.at[pl.ds(first, 2)]
        return remote(here, here, agx.at[0], agx.at[1], opposite)

    x_copy(2 * r).start()
    for way in range(2):
        z_copy(0, way, 0, 2 * r, 2).start()
    p_copy(0, 0).start()

    def gather_x():
        first = shard(1, 0)
        x_copy(first).wait_recv()
        for way in range(2):
            z_copy(1, way, 0, first, 2).start()
        p_copy(1, 0).start()

    def gather_step(st, s):
        for way in range(2):
            o = -s if way == 0 else s
            first = shard(st, o)
            if s < 4:
                z_copy(st, way, s - 1, first, 2).wait_recv()
                if s < 3:
                    z_copy(st, way, s, first, 2).start()
                else:
                    z_copy(st, way, s, first + way, 1).start()
                p_copy(st, o).start()
            else:
                z_copy(st, way, s - 1, first + way, 1).wait_recv()
        if s == 4:
            p_copy(st, 4).start()

    gather_x()
    gather_step(0, 1)
    gather_step(1, 1)
    gather_step(0, 2)

    for i in range(1, NCOL):
        col_copy(i, crel(-i)).wait_recv()

    weight = w[...]
    for b in range(ROW_BLOCKS):
        gagg[b] = lax.dot_general(
            weight, gbuf[b], (((1,), (1,)), ((), ())), preferred_element_type=jnp.float32
        ).astype(jnp.bfloat16)
    for copy in tile_copies:
        copy.wait()

    def tile_step(base, i, acc, product):
        terms = []
        for u in range(UNROLL):
            v = plan[base + i * UNROLL + u]
            terms.append(product((v // 256) % 256, v % 256))
        for u in range(UNROLL):
            k = i * UNROLL + u
            here = plan[base + k] // 65536
            before = plan[base + jnp.maximum(k - 1, 0)] // 65536
            keep = jnp.where(here == before, 1.0, 0.0)
            acc = acc * keep + terms[u]
            runs[k] = acc
        return acc

    def backward(t, o):
        return jnp.dot(gagg[o], tv[t], preferred_element_type=jnp.float32)

    def forward(t, o):
        return jnp.dot(tv[t], fbuf[o], preferred_element_type=jnp.float32)

    def backward_body(i, acc):
        for at, st, s in ((1, 1, 2), (3, 0, 3), (6, 1, 3)):
            @pl.when(i == at)
            def _(st=st, s=s):
                gather_step(st, s)
        return tile_step(B_ORDER, i, acc, backward)

    zero = jnp.zeros((TB, F), jnp.float32)
    lax.fori_loop(0, STEPS, backward_body, zero)

    def extract(which, first, size):
        k = 1 - core if which == 0 else core

        def body(q, carry):
            j = q // 4
            rel = lax.rem(q // 2, 2)
            blk = lax.rem(q, 2)
            o = jnp.where(
                j == 0, 4, jnp.where(j == 7, 0, jnp.where(lax.rem(j, 2) == 1, 3 - j // 2, 4 + j // 2))
            )
            a = jnp.where(rel == 1, xh, 1 - xh)
            b = 2 * rid(a, lax.rem(z + o, NZ), k) + blk
            part[which, j, rel, blk] = runs[plan[B_LAST + b]].astype(jnp.bfloat16)
            return carry

        lax.fori_loop(4 * first, 4 * (first + size), body, 0)

    def peer_copy(n):
        first, size = PIECES[n]
        return remote(
            part.at[0, pl.ds(first, size)], peer.at[pl.ds(first, size)],
            rp_s.at[n], rp_r.at[n], partner,
        )

    for n, (first, size) in enumerate(PIECES):
        extract(0, first, size)
        peer_copy(n).start()
    extract(1, 0, NZ)

    gather_step(0, 4)
    gather_step(1, 4)

    def ring_copy(way, t, rel):
        if t == 0:
            src, dst = ring_out.at[way, t, rel, way], ring_in.at[way, t, rel, way]
        else:
            src, dst = ring_out.at[way, t, rel], ring_in.at[way, t, rel]
        return remote(
            src, dst, rz_s.at[way, t, rel], rz_r.at[way, t, rel], up if way == 0 else down
        )

    def own(j, rel, blk):
        return part[1, j, rel, blk].astype(jnp.float32) + peer[j, rel, blk].astype(jnp.float32)

    def ring_step(t):
        peer_copy(t).wait_recv()
        for rel in range(2):
            for way in range(2):
                j = 0 if t == 0 else 2 * t - 1 + way
                if t > 0:
                    ring_copy(way, t - 1, rel).wait_recv()
                for blk in range(2):
                    if t == 0 and blk != way:
                        continue
                    value = own(j, rel, blk)
                    if t > 1 or (t == 1 and blk == way):
                        value = value + ring_in[way, t - 1, rel, blk].astype(jnp.float32)
                    ring_out[way, t, rel, blk] = value.astype(jnp.bfloat16)
                ring_copy(way, t, rel).start()

    def ring_end(rel):
        total = []
        for way in range(2):
            ring_copy(way, 3, rel).wait_recv()
        for blk in range(2):
            total.append(
                own(7, rel, blk)
                + ring_in[0, 3, rel, blk].astype(jnp.float32)
                + ring_in[1, 3, rel, blk].astype(jnp.float32)
            )
        return total

    ring_step(0)

    for st in range(2):
        for o in range(NZ):
            p_copy(st, o, mine=False).wait_recv()

    def forward_body(i, acc):
        @pl.when(i == 5)
        def _():
            ring_step(1)

        return tile_step(F_ORDER, i, acc, forward)

    lax.fori_loop(0, STEPS, forward_body, zero)

    for b in range(ROW_BLOCKS):
        agg[b] = runs[plan[F_LAST + b]].astype(jnp.bfloat16)

    def agg_copy(i):
        return remote(
            agg.at[pl.ds(2 * crel(i), 2)], agg_in.at[i - 1], cr_s.at[i - 1], cr_r.at[i - 1], cpeer[i]
        )

    for i in range(1, NCOL):
        agg_copy(i).start()

    term = lax.dot_general(
        agg[...].reshape(ROW_BLOCKS * TB, F), gbuf[...].reshape(ROW_BLOCKS * TB, F),
        (((0,), (0,)), ((), ())), preferred_element_type=jnp.float32,
    )
    wt[...] = term.reshape(NCOL, F // NCOL, F)

    def red1_copy(i):
        return remote(wt.at[crel(i)], red1.at[i - 1], a1_s.at[i - 1], a1_r.at[i - 1], cpeer[i])

    quad = xh * 2 + core
    quad_peer = (None, partner, opposite, diagonal)

    def quad_of(i):
        k = core if i % 2 == 0 else 1 - core
        return (xh if i < 2 else 1 - xh) * 2 + k

    def red2_copy(i, owner):
        here = red2.at[owner]
        return remote(here, here, a2_s.at[i - 1], a2_r.at[i - 1], quad_peer[i])

    def red3_copy(i, owner):
        here = red3.at[owner]
        return remote(here, here, a3_s.at[i - 1], a3_r.at[i - 1], zpeer[i])

    def red4_copy(i, owner):
        here = red4.at[owner]
        return remote(here, here, a4_s.at[i - 1], a4_r.at[i - 1], cpeer[i])

    for i in range(1, NCOL):
        red1_copy(i).start()

    ring_step(2)

    for i in range(1, NCOL):
        red1_copy(i).wait_recv()
    total = wt[c]
    for i in range(NCOL - 1):
        total = total + red1[i]
    red2[quad] = total
    for i in range(1, 4):
        red2_copy(i, quad).start()

    for i in range(1, NCOL):
        agg_copy(i).wait_recv()
    for blk in range(2):
        total = agg[2 * c + blk].astype(jnp.float32)
        for i in range(NCOL - 1):
            total = total + agg_in[i, blk].astype(jnp.float32)
        lay_ref[blk] = jnp.dot(
            total.astype(jnp.bfloat16), w[...], preferred_element_type=jnp.float32
        ).astype(jnp.bfloat16)

    ring_step(3)

    for i in range(1, 4):
        red2_copy(i, quad_of(i)).wait_recv()
    red3[z] = red2[0] + red2[1] + red2[2] + red2[3]
    for i in range(1, NZ):
        red3_copy(i, z).start()

    peer_copy(4).wait_recv()
    out = ring_end(0)
    for blk in range(2):
        x_out[blk] = out[blk].astype(jnp.bfloat16)
    last_copy = remote(x_out, x_in, rx.at[0], rx.at[1], opposite)
    last_copy.start()

    for i in range(1, NZ):
        red3_copy(i, zrel(-i)).wait_recv()
    total = red3[0]
    for i in range(1, NZ):
        total = total + red3[i]
    red4[c] = total * (1.0 / math.sqrt(65536))
    for i in range(1, NCOL):
        red4_copy(i, c).start()

    out = ring_end(1)
    last_copy.wait_recv()
    for blk in range(2):
        total = out[blk] + x_in[blk].astype(jnp.float32)
        gf_ref[blk] = total.T.astype(jnp.bfloat16)

    for i in range(1, NCOL):
        red4_copy(i, crel(-i)).wait_recv()
    gw_ref[...] = red4[...].reshape(F, F)

    for i in range(1, NCOL):
        col_copy(i, c).wait_send()
        agg_copy(i).wait_send()
        red1_copy(i).wait_send()
        red3_copy(i, z).wait_send()
        red4_copy(i, c).wait_send()
    for i in range(1, 4):
        red2_copy(i, quad).wait_send()
    x_copy(2 * r).wait_send()
    last_copy.wait_send()
    for n in range(len(PIECES)):
        peer_copy(n).wait_send()
    for st in range(2):
        for o in range(NZ):
            p_copy(st, o).wait_send()
        for way in range(2):
            for step in range(4):
                z_copy(st, way, step, shard(st, 0), 2 if step < 3 else 1).wait_send()
                ring_copy(way, step, st).wait_send()


def per_device(features, tiles, tile_rows, tile_cols, tile_count, weight, grad_out):
    plan = tile_plan(tile_rows[0, 0], tile_cols[0, 0], tile_count[0, 0])
    bf, f32 = jnp.bfloat16, jnp.float32
    dma = pltpu.SemaphoreType.DMA
    vmem = pl.BlockSpec(memory_space=pltpu.VMEM)
    lay, gf, gw = pl.pallas_call(
        kernel,
        out_shape=(
            jax.ShapeDtypeStruct((2, TB, F), bf),
            jax.ShapeDtypeStruct((2, TB, F), bf),
            jax.ShapeDtypeStruct((F, F), f32),
        ),
        in_specs=[
            pl.BlockSpec(memory_space=pltpu.SMEM), vmem, vmem, vmem,
            pl.BlockSpec(memory_space=pl.ANY),
        ],
        out_specs=(vmem, vmem, vmem),
        scratch_shapes=[
            pltpu.VMEM((SLOTS, TB, TB), bf),
            pltpu.VMEM((COL_BLOCKS, TB, F), bf),
            pltpu.VMEM((ROW_BLOCKS, TB, F), bf),
            pltpu.VMEM((ROW_BLOCKS, F, TB), bf),
            pltpu.VMEM((SLOTS + 1, TB, F), f32),
            pltpu.VMEM((2, NZ, 2, 2, F, TB), bf),
            pltpu.VMEM((NZ, 2, 2, F, TB), bf),
            pltpu.VMEM((2, 4, 2, 2, F, TB), bf),
            pltpu.VMEM((2, 4, 2, 2, F, TB), bf),
            pltpu.VMEM((2, F, TB), bf),
            pltpu.VMEM((2, F, TB), bf),
            pltpu.VMEM((ROW_BLOCKS, TB, F), bf),
            pltpu.VMEM((NCOL - 1, 2, TB, F), bf),
            pltpu.VMEM((NCOL, F // NCOL, F), f32),
            pltpu.VMEM((NCOL - 1, F // NCOL, F), f32),
            pltpu.VMEM((4, F // NCOL, F), f32),
            pltpu.VMEM((NZ, F // NCOL, F), f32),
            pltpu.VMEM((NCOL, F // NCOL, F), f32),
            dma((4,)), dma((7,)), dma((7,)), dma((2, 2, 4)), dma((2, 2, 4)), dma((2,)),
            dma((2, NZ)), dma((2, NZ)), dma((5,)), dma((5,)), dma((2, 4, 2)), dma((2, 4, 2)),
            dma((2,)), dma((7,)), dma((7,)), dma((7,)), dma((7,)), dma((3,)), dma((3,)),
            dma((7,)), dma((7,)), dma((7,)), dma((7,)),
        ],
        compiler_params=pltpu.CompilerParams(
            collective_id=0, has_side_effects=True, vmem_limit_bytes=48 * 2**20
        ),
        cost_estimate=pl.CostEstimate(flops=2 * 2 * SLOTS * TB * TB * F, bytes_accessed=2**23, transcendentals=0),
        name="aggregate",
    )(
        plan,
        features.reshape(2, TB, F),
        grad_out.reshape(2, TB, F),
        weight,
        tiles.reshape(SLOTS, TB, TB),
    )
    return (lay.reshape(1, 2 * TB, F), gf.reshape(1, 2 * TB, F), gw)


def solution(mesh):
    in_specs = (
        P("col", "row", None),
        P("row", "col", None, None, None),
        P("row", "col", None),
        P("row", "col", None),
        P("row", "col"),
        P(),
        P("row", "col", None),
    )
    out_specs = (P("row", "col", None), P("col", "row", None), P())
    return jax.shard_map(
        per_device, mesh=mesh, in_specs=in_specs, out_specs=out_specs, check_vma=False
    )
```

```python
import math

import jax
import jax.numpy as jnp
from jax import lax
from jax.experimental import pallas as pl
from jax.experimental.pallas import tpu as pltpu
from jax.sharding import PartitionSpec as P

TB = 128
F = 128
SLOTS = 256
ROW_BLOCKS = 16
COL_BLOCKS = 64
NZ = 8
NCOL = 8
UNROLL = 32
STEPS = SLOTS // UNROLL
EMPTY = SLOTS
KEY_BITS = 16
SLOT_BITS = 8
OFFSETS = (4, 3, 5, 2, 6, 1, 7, 0)
PIECES = ((0, 1), (1, 2), (3, 2), (5, 3))
NEXT, SECOND, THIRD, FOURTH, NEXT_B = range(5)
B_ORDER, B_LAST, F_ORDER, F_LAST = range(4)


def remote(src, dst, send, recv, device):
    return pltpu.make_async_remote_copy(
        src_ref=src, dst_ref=dst, send_sem=send, recv_sem=recv,
        device_id=device, device_id_type=pl.DeviceIdType.MESH,
    )


def sorted_plan(key, other, count):
    lane = lax.broadcasted_iota(jnp.int32, (1, SLOTS), 1)
    key = jnp.where(lane < count, key, COL_BLOCKS)
    value = (key * 2**KEY_BITS + lane * 2**SLOT_BITS + other).astype(jnp.float32)
    across = lax.broadcasted_iota(jnp.int32, (SLOTS, SLOTS), 1)
    along = lax.broadcasted_iota(jnp.int32, (SLOTS, SLOTS), 0)
    column = jnp.sum(jnp.where(across == along, value, 0.0), axis=1, keepdims=True)
    place = jnp.sum(jnp.where(value < column, 1.0, 0.0), axis=1, keepdims=True)
    order = jnp.sum(jnp.where(place == across.astype(jnp.float32), column, 0.0), axis=0, keepdims=True)
    bound = (lane * 2**KEY_BITS).astype(jnp.float32)
    below = jnp.sum(jnp.where(column < bound, 1.0, 0.0), axis=0, keepdims=True)
    upto = jnp.sum(jnp.where(column < bound + 2.0**KEY_BITS, 1.0, 0.0), axis=0, keepdims=True)
    last = jnp.where(upto > below, upto - 1.0, float(EMPTY))
    return order.astype(jnp.int32), last.astype(jnp.int32)


def kernel(
    count, rows_hbm, cols_hbm, feat_hbm, gout_hbm, w_hbm, tiles_hbm, lay_ref, gf_ref, gw_ref,
    rows, cols, gin, w, plan_v, plan,
    tv, fbuf, gbuf, runs, part, peer, x_out, x_in, z_out, z_in,
    agg, agg_in, wt, red1, red2, red3, red4,
    load, tile_sem, plan_sem, col_s, col_r, agz_s, agz_r, agx_s, agx_r, agp_s, agp_r,
    rp_s, rp_r, rx_s, rx_r, rz_s, rz_r, cr_s, cr_r,
    a1_s, a1_r, a2_s, a2_r, a3_s, a3_r, a4_s, a4_r,
):
    r = lax.axis_index("row")
    c = lax.axis_index("col")
    core = lax.rem(r, 2)
    z = lax.rem(r // 2, NZ)
    xh = r // (2 * NZ)

    def rid(a, b, k):
        return (a * NZ + b) * 2 + k

    def zrel(o):
        return lax.rem(z + (o % NZ), NZ)

    def crel(o):
        return lax.rem(c + (o % NCOL), NCOL)

    def cid(yo, near):
        side = lax.rem(c, 2)
        return 2 * lax.rem(c // 2 + (yo % 4), 4) + (side if near == 0 else 1 - side)

    partner = (rid(xh, z, 1 - core), c)
    opposite = (rid(1 - xh, z, core), c)
    diagonal = (rid(1 - xh, z, 1 - core), c)
    beside = (r, cid(0, 1))
    ypeer = [None] + [(r, cid(i, 0)) for i in range(1, 4)]
    zpeer = [None] + [(rid(xh, zrel(i), core), c) for i in range(1, NZ)]
    cpeer = [None] + [(r, crel(i)) for i in range(1, NCOL)]
    far_first = (4, 3, 5, 2, 6, 1, 7)

    loads = [
        pltpu.make_async_copy(src, dst, load.at[i])
        for i, (src, dst) in enumerate(
            (
                (gout_hbm, gin),
                (feat_hbm, fbuf.at[pl.ds(2 * r, 2)]),
                (rows_hbm, rows),
                (cols_hbm, cols),
                (w_hbm, w),
            )
        )
    ]
    tile_copies = [
        pltpu.make_async_copy(
            tiles_hbm.at[pl.ds(64 * i, 64)], tv.at[pl.ds(64 * i, 64)], tile_sem.at[i]
        )
        for i in range(4)
    ]
    for copy in loads:
        copy.start()
    for copy in tile_copies:
        copy.start()
    barrier = pltpu.get_barrier_semaphore()
    everyone = zpeer[1:] + cpeer[1:] + [partner, opposite, diagonal]
    for device in everyone:
        pl.semaphore_signal(
            barrier, inc=1, device_id=device, device_id_type=pl.DeviceIdType.MESH
        )
    runs[EMPTY] = jnp.zeros((TB, F), jnp.float32)
    loads[0].wait()
    for blk in range(2):
        gbuf[2 * c + blk] = gin[blk].astype(jnp.float32).T.astype(jnp.bfloat16)
    loads[1].wait()
    pl.semaphore_wait(barrier, len(everyone))

    def col_shard(yo, near):
        return gbuf.at[pl.ds(2 * cid(yo, near), 2)]

    def col_copy(i, near, yo):
        here = col_shard(yo, near)
        return remote(here, here, col_s.at[near, i], col_r.at[near, i], ypeer[i])

    def side_copy(near):
        here = col_shard(0, near)
        return remote(here, here, col_s.at[0, 0], col_r.at[0, 0], beside)

    def shard(st, o, k):
        return fbuf.at[pl.ds(2 * rid(xh if st == 0 else 1 - xh, zrel(o), k), 2)]

    def z_copy(kind, way, o):
        sign = 1 if way == 0 else -1
        here = shard(1 if kind == NEXT_B else 0, o, core)
        if kind == FOURTH:
            here = fbuf.at[pl.ds(2 * rid(xh, zrel(o), core) + way, 1)]
        step = 2 if kind in (SECOND, FOURTH) else 1
        return remote(
            here, here, agz_s.at[kind, way], agz_r.at[kind, way], zpeer[(sign * step) % NZ]
        )

    def x_copy(o, st):
        here = shard(st, o, core)
        return remote(here, here, agx_s.at[o % NZ], agx_r.at[o % NZ], opposite)

    def p_copy(st, o, k):
        here = shard(st, o, k)
        return remote(here, here, agp_s.at[st, o % NZ], agp_r.at[st, o % NZ], partner)

    side_copy(0).start()
    for i in (2, 1, 3):
        col_copy(i, 0, 0).start()
    x_copy(0, 0).start()
    for kind in (SECOND, NEXT):
        for way in range(2):
            z_copy(kind, way, 0).start()
    p_copy(0, 0, core).start()

    def arrive_z(kind, way):
        back = (1, 2, 3, 4, 1)[kind]
        o = -back if way == 0 else back
        z_copy(kind, way, o).wait_recv()
        if kind == SECOND:
            z_copy(THIRD, way, o).start()
            z_copy(FOURTH, way, o).start()
        if kind in (SECOND, THIRD):
            x_copy(o, 0).start()
        if kind == FOURTH:
            if way == 0:
                return
            x_copy(4, 0).start()
        p_copy(1 if kind == NEXT_B else 0, o, core).start()

    def arrive_x(o):
        x_copy(o, 1).wait_recv()
        if o == 0:
            for way in range(2):
                z_copy(NEXT_B, way, 0).start()
        p_copy(1, o, core).start()

    def arrive_side():
        side_copy(1).wait_recv()
        for i in (2, 1, 3):
            col_copy(i, 1, 0).start()

    arrive_side()
    arrive_x(0)
    for way in range(2):
        arrive_z(NEXT, way)

    loads[2].wait()
    loads[3].wait()
    live = count[0, 0]
    order, last = sorted_plan(cols[...], rows[...], live)
    plan_v[pl.ds(B_ORDER, 1)] = order
    plan_v[pl.ds(B_LAST, 1)] = last
    order, last = sorted_plan(rows[...], cols[...], live)
    plan_v[pl.ds(F_ORDER, 1)] = order
    plan_v[pl.ds(F_LAST, 1)] = last
    plan_copy = pltpu.make_async_copy(plan_v, plan, plan_sem.at[0])
    plan_copy.start()

    for way in range(2):
        arrive_z(SECOND, way)

    plan_copy.wait()
    for copy in tile_copies:
        copy.wait()
    loads[4].wait()
    for near in range(2):
        for i in range(1, 4):
            col_copy(i, near, -i).wait_recv()

    def tile_step(which, i, acc, product):
        value = [plan[which, i * UNROLL + u] for u in range(UNROLL)]
        before = [plan[which, jnp.maximum(i * UNROLL - 1, 0)]] + value[:-1]
        terms = []
        for v in value:
            terms.append(product((v >> SLOT_BITS) & (SLOTS - 1), v))
        for u in range(UNROLL):
            same = (value[u] >> KEY_BITS) == (before[u] >> KEY_BITS)
            acc = acc * jnp.where(same, 1.0, 0.0) + terms[u]
            runs[i * UNROLL + u] = acc
        return acc

    def final_run(which, block):
        last = jnp.clip(plan[which, block], 0, EMPTY)
        return runs[last].astype(jnp.bfloat16)

    def backward(t, o):
        return jnp.dot(gbuf[o & (ROW_BLOCKS - 1)], tv[t], preferred_element_type=jnp.float32)

    def forward(t, o):
        return jnp.dot(tv[t], fbuf[o & (COL_BLOCKS - 1)], preferred_element_type=jnp.float32)

    def backward_body(i, acc):
        @pl.when(i == 0)
        def _():
            for way in range(2):
                arrive_z(THIRD, way)

        @pl.when(i == 2)
        def _():
            for way in range(2):
                arrive_z(FOURTH, way)
                arrive_z(NEXT_B, way)

        @pl.when(i == 5)
        def _():
            arrive_x(2)
            arrive_x(6)

        return tile_step(B_ORDER, i, acc, backward)

    zero = jnp.zeros((TB, F), jnp.float32)
    lax.fori_loop(0, STEPS, backward_body, zero)

    def block_of(which, j, rel):
        k = 1 - core if which == 0 else core
        o = jnp.where(
            j == 0, 4, jnp.where(j == 7, 0, jnp.where(lax.rem(j, 2) == 1, 3 - j // 2, 4 + j // 2))
        )
        a = jnp.where(rel == 1, xh, 1 - xh)
        return 2 * rid(a, lax.rem(z + o, NZ), k)

    def extract(which, first, size):
        def body(q, carry):
            j = q // 2
            rel = lax.rem(q, 2)
            b = block_of(which, j, rel)
            for blk in range(2):
                part[which, j, rel, blk] = final_run(B_LAST, b + blk)
            return carry

        lax.fori_loop(2 * first, 2 * (first + size), body, 0)

    def peer_copy(n):
        first, size = PIECES[n]
        return remote(
            part.at[0, pl.ds(first, size)], peer.at[pl.ds(first, size)],
            rp_s.at[n], rp_r.at[n], partner,
        )

    def rx_copy(o):
        return remote(x_out.at[o], x_in.at[o], rx_s.at[o], rx_r.at[o], opposite)

    def rz_copy(kind, way):
        sign = 1 if way == 0 else -1
        src, dst = z_out.at[kind, way], z_in.at[kind, way]
        if kind == FOURTH:
            src, dst = z_out.at[kind, way, way], z_in.at[kind, way, way]
        step = 2 if kind in (SECOND, FOURTH) else 1
        return remote(src, dst, rz_s.at[kind, way], rz_r.at[kind, way], zpeer[(sign * step) % NZ])

    def own(j, rel, blk):
        return part[1, j, rel, blk].astype(jnp.float32) + peer[j, rel, blk].astype(jnp.float32)

    for n, (first, size) in enumerate(PIECES):
        extract(0, first, size)
        peer_copy(n).start()
    extract(1, 0, NZ)
    place = {o: j for j, o in enumerate(OFFSETS)}

    def send_x(o):
        for blk in range(2):
            value = own(place[o], 0, blk)
            if o == 0:
                for way in range(2):
                    value = value + z_in[NEXT_B, way, blk].astype(jnp.float32)
            x_out[o, blk] = value.astype(jnp.bfloat16)
        rx_copy(o).start()

    def send_z(kind, way):
        o = (1, 2, 3, 4, 1)[kind] * (1 if way == 0 else -1) % NZ
        rel = 0 if kind == NEXT_B else 1
        if kind in (SECOND, THIRD) or (kind == FOURTH and way == 0):
            rx_copy(o).wait_recv()
        if kind == SECOND:
            for other in (THIRD, FOURTH):
                rz_copy(other, way).wait_recv()
        for blk in range(2):
            if kind == FOURTH and blk != way:
                continue
            value = own(place[o], rel, blk)
            if kind in (SECOND, THIRD, FOURTH):
                value = value + x_in[o, blk].astype(jnp.float32)
            if kind == SECOND:
                value = value + z_in[THIRD, way, blk].astype(jnp.float32)
                if blk == way:
                    value = value + z_in[FOURTH, way, blk].astype(jnp.float32)
            z_out[kind, way, blk] = value.astype(jnp.bfloat16)
        rz_copy(kind, way).start()

    for n in range(len(PIECES)):
        peer_copy(n).wait_recv()
        for o in ((4,), (3, 5), (2, 6), ())[n]:
            send_x(o)
    for kind in (NEXT_B, NEXT):
        for way in range(2):
            send_z(kind, way)

    for o in (3, 5, 4):
        arrive_x(o)
    for st in range(2):
        for o in range(NZ):
            p_copy(st, o, 1 - core).wait_recv()

    def term_body(j, acc):
        for which in range(2):
            for rel in range(2):
                b = block_of(which, j, rel)
                left = jnp.concatenate([part[which, j, rel, 0], part[which, j, rel, 1]], axis=1)
                right = fbuf[pl.ds(b, 2)].reshape(2 * TB, F)
                acc = acc + jnp.dot(left, right, preferred_element_type=jnp.float32)
        return acc

    term = lax.fori_loop(0, NZ, term_body, zero)
    wt[...] = term.reshape(NCOL, F // NCOL, F)

    def red1_copy(i):
        return remote(wt.at[crel(i)], red1.at[i - 1], a1_s.at[i - 1], a1_r.at[i - 1], cpeer[i])

    quad = xh * 2 + core
    quad_peer = (None, partner, opposite, diagonal)

    def quad_of(i):
        k = core if i % 2 == 0 else 1 - core
        return (xh if i < 2 else 1 - xh) * 2 + k

    def red2_copy(i, owner):
        here = red2.at[owner]
        return remote(here, here, a2_s.at[i - 1], a2_r.at[i - 1], quad_peer[i])

    def red3_copy(i, owner):
        here = red3.at[owner]
        return remote(here, here, a3_s.at[i - 1], a3_r.at[i - 1], zpeer[i])

    def red4_copy(i, owner):
        here = red4.at[owner]
        return remote(here, here, a4_s.at[i - 1], a4_r.at[i - 1], cpeer[i])

    for i in (5, 3, 4, 6, 2, 7, 1):
        red1_copy(i).start()

    lax.fori_loop(0, STEPS, lambda i, acc: tile_step(F_ORDER, i, acc, forward), zero)

    for b in range(ROW_BLOCKS):
        agg[b] = final_run(F_LAST, b)

    def agg_copy(i):
        return remote(
            agg.at[pl.ds(2 * crel(i), 2)], agg_in.at[i - 1], cr_s.at[i - 1], cr_r.at[i - 1], cpeer[i]
        )

    for i in (5, 3, 4, 6, 2, 7, 1):
        agg_copy(i).start()

    for way in range(2):
        send_z(FOURTH, way)
    for way in range(2):
        send_z(THIRD, way)
    for way in range(2):
        rz_copy(NEXT_B, way).wait_recv()
    send_x(0)

    for i in range(1, NCOL):
        red1_copy(i).wait_recv()
    total = wt[c]
    for i in range(NCOL - 1):
        total = total + red1[i]
    red2[quad] = total
    for i in (3, 2, 1):
        red2_copy(i, quad).start()

    for i in range(1, 4):
        red2_copy(i, quad_of(i)).wait_recv()
    red3[z] = red2[0] + red2[1] + red2[2] + red2[3]
    for i in far_first:
        red3_copy(i, z).start()

    for way in range(2):
        send_z(SECOND, way)

    for i in range(1, NCOL):
        agg_copy(i).wait_recv()
    for blk in range(2):
        total = agg[2 * c + blk].astype(jnp.float32)
        for i in range(NCOL - 1):
            total = total + agg_in[i, blk].astype(jnp.float32)
        lay_ref[blk] = jnp.dot(
            total.astype(jnp.bfloat16), w[...], preferred_element_type=jnp.float32
        ).astype(jnp.bfloat16)

    for i in range(1, NZ):
        red3_copy(i, zrel(-i)).wait_recv()
    total = red3[0]
    for i in range(1, NZ):
        total = total + red3[i]
    red4[c] = total * (1.0 / math.sqrt(65536))
    for i in (5, 3, 4, 6, 2, 7, 1):
        red4_copy(i, c).start()

    rx_copy(0).wait_recv()
    for kind in (NEXT, SECOND):
        for way in range(2):
            rz_copy(kind, way).wait_recv()
    for blk in range(2):
        total = own(place[0], 1, blk) + x_in[0, blk].astype(jnp.float32)
        for kind in (NEXT, SECOND):
            for way in range(2):
                total = total + z_in[kind, way, blk].astype(jnp.float32)
        upper = total.astype(jnp.bfloat16)
        lower = (total - upper.astype(jnp.float32)).astype(jnp.bfloat16)
        value = jnp.zeros((TB, F), jnp.float32)
        for share in (lower, upper):
            value = value + lax.dot_general(
                share, w[...], (((0,), (1,)), ((), ())), preferred_element_type=jnp.float32
            )
        gf_ref[blk] = value.astype(jnp.bfloat16)

    for i in range(1, NCOL):
        red4_copy(i, crel(-i)).wait_recv()
    gw_ref[...] = red4[...].reshape(F, F).T

    side_copy(0).wait_send()
    for i in range(1, NCOL):
        agg_copy(i).wait_send()
        red1_copy(i).wait_send()
        red3_copy(i, z).wait_send()
        red4_copy(i, c).wait_send()
    for near in range(2):
        for i in range(1, 4):
            col_copy(i, near, 0).wait_send()
    for i in range(1, 4):
        red2_copy(i, quad).wait_send()
    for n in range(len(PIECES)):
        peer_copy(n).wait_send()
    for kind in range(5):
        for way in range(2):
            z_copy(kind, way, 0).wait_send()
            rz_copy(kind, way).wait_send()
    for o in (0, 2, 3, 4, 5, 6):
        x_copy(o, 0).wait_send()
        rx_copy(o).wait_send()
    for st in range(2):
        for o in range(NZ):
            p_copy(st, o, core).wait_send()


def per_device(features, tiles, tile_rows, tile_cols, tile_count, weight, grad_out):
    bf, f32, i32 = jnp.bfloat16, jnp.float32, jnp.int32
    dma = pltpu.SemaphoreType.DMA
    vmem = pl.BlockSpec(memory_space=pltpu.VMEM)
    anywhere = pl.BlockSpec(memory_space=pl.ANY)
    pair = (2, TB, F)
    out_shape = (
        jax.ShapeDtypeStruct(pair, bf),
        jax.ShapeDtypeStruct(pair, bf),
        jax.ShapeDtypeStruct((F, F), f32),
    )
    lay, gf, gw = pl.pallas_call(
        kernel,
        out_shape=out_shape,
        in_specs=[pl.BlockSpec(memory_space=pltpu.SMEM)] + [anywhere] * 6,
        out_specs=(vmem, vmem, vmem),
        scratch_shapes=[
            pltpu.VMEM((1, SLOTS), i32),
            pltpu.VMEM((1, SLOTS), i32),
            pltpu.VMEM(pair, bf),
            pltpu.VMEM((F, F), bf),
            pltpu.VMEM((4, SLOTS), i32),
            pltpu.SMEM((4, SLOTS), i32),
            pltpu.VMEM((SLOTS, TB, TB), bf),
            pltpu.VMEM((COL_BLOCKS, TB, F), bf),
            pltpu.VMEM((ROW_BLOCKS, F, TB), bf),
            pltpu.VMEM((SLOTS + 1, TB, F), f32),
            pltpu.VMEM((2, NZ, 2, 2, F, TB), bf),
            pltpu.VMEM((NZ, 2, 2, F, TB), bf),
            pltpu.VMEM((NZ, 2, F, TB), bf),
            pltpu.VMEM((NZ, 2, F, TB), bf),
            pltpu.VMEM((5, 2, 2, F, TB), bf),
            pltpu.VMEM((5, 2, 2, F, TB), bf),
            pltpu.VMEM((ROW_BLOCKS, TB, F), bf),
            pltpu.VMEM((NCOL - 1, 2, TB, F), bf),
            pltpu.VMEM((NCOL, F // NCOL, F), f32),
            pltpu.VMEM((NCOL - 1, F // NCOL, F), f32),
            pltpu.VMEM((4, F // NCOL, F), f32),
            pltpu.VMEM((NZ, F // NCOL, F), f32),
            pltpu.VMEM((NCOL, F // NCOL, F), f32),
            dma((5,)), dma((4,)), dma((1,)), dma((2, 4)), dma((2, 4)), dma((5, 2)), dma((5, 2)),
            dma((NZ,)), dma((NZ,)), dma((2, NZ)), dma((2, NZ)),
            dma((4,)), dma((4,)), dma((NZ,)), dma((NZ,)), dma((5, 2)), dma((5, 2)), dma((7,)), dma((7,)),
            dma((7,)), dma((7,)), dma((3,)), dma((3,)), dma((7,)), dma((7,)), dma((7,)), dma((7,)),
        ],
        compiler_params=pltpu.CompilerParams(
            collective_id=0, has_side_effects=True, vmem_limit_bytes=63 * 2**20
        ),
        cost_estimate=pl.CostEstimate(
            flops=4 * SLOTS * TB * TB * F, bytes_accessed=2**23, transcendentals=0
        ),
        name="aggregate",
    )(
        tile_count,
        tile_rows.reshape(1, SLOTS),
        tile_cols.reshape(1, SLOTS),
        features.reshape(pair),
        grad_out.reshape(pair),
        weight,
        tiles.reshape(SLOTS, TB, TB),
    )
    return (lay.reshape(1, 2 * TB, F), gf.reshape(1, 2 * TB, F), gw)


def solution(mesh):
    in_specs = (
        P("col", "row", None),
        P("row", "col", None, None, None),
        P("row", "col", None),
        P("row", "col", None),
        P("row", "col"),
        P(),
        P("row", "col", None),
    )
    out_specs = (P("row", "col", None), P("col", "row", None), P())
    return jax.shard_map(
        per_device, mesh=mesh, in_specs=in_specs, out_specs=out_specs, check_vma=False
    )
```

```python
import math

import jax
import jax.numpy as jnp
from jax import lax
from jax.experimental import pallas as pl
from jax.experimental.pallas import tpu as pltpu
from jax.sharding import PartitionSpec as P

TB = 128
F = 128
SLOTS = 256
ROW_BLOCKS = 16
COL_BLOCKS = 64
NZ = 8
NCOL = 8
UNROLL = 32
STEPS = SLOTS // UNROLL
EMPTY = SLOTS
KEY_BITS = 16
SLOT_BITS = 8
OFFSETS = (4, 3, 5, 2, 6, 1, 7, 0)
PIECES = ((0, 1), (1, 2), (3, 2), (5, 3))
NEXT, SECOND, THIRD, FOURTH, NEXT_B = range(5)
B_ORDER, B_LAST, F_ORDER, F_LAST = range(4)


def remote(src, dst, send, recv, device):
    return pltpu.make_async_remote_copy(
        src_ref=src, dst_ref=dst, send_sem=send, recv_sem=recv,
        device_id=device, device_id_type=pl.DeviceIdType.MESH,
    )


def sorted_plan(key, other, count):
    lane = lax.broadcasted_iota(jnp.int32, (1, SLOTS), 1)
    key = jnp.where(lane < count, key, COL_BLOCKS)
    value = (key * 2**KEY_BITS + lane * 2**SLOT_BITS + other).astype(jnp.float32)
    across = lax.broadcasted_iota(jnp.int32, (SLOTS, SLOTS), 1)
    along = lax.broadcasted_iota(jnp.int32, (SLOTS, SLOTS), 0)
    column = jnp.sum(jnp.where(across == along, value, 0.0), axis=1, keepdims=True)
    place = jnp.sum(jnp.where(value < column, 1.0, 0.0), axis=1, keepdims=True)
    order = jnp.sum(jnp.where(place == across.astype(jnp.float32), column, 0.0), axis=0, keepdims=True)
    bound = (lane * 2**KEY_BITS).astype(jnp.float32)
    below = jnp.sum(jnp.where(column < bound, 1.0, 0.0), axis=0, keepdims=True)
    upto = jnp.sum(jnp.where(column < bound + 2.0**KEY_BITS, 1.0, 0.0), axis=0, keepdims=True)
    last = jnp.where(upto > below, upto - 1.0, float(EMPTY))
    return order.astype(jnp.int32), last.astype(jnp.int32)


def kernel(
    count, rows_hbm, cols_hbm, feat_hbm, gout_hbm, w_hbm, tiles_hbm, lay_ref, gf_ref, gw_ref,
    rows, cols, gin, w, plan_v, plan,
    tv, fbuf, gbuf, runs, part, peer, x_out, x_in, z_out, z_in,
    agg, agg_in, wt, red1, red2, red3,
    load, tile_sem, plan_sem, col_s, col_r, agz_s, agz_r, agx_s, agx_r, agp_s, agp_r,
    rp_s, rp_r, rx_s, rx_r, rz_s, rz_r, cr_s, cr_r,
    a1_s, a1_r, a2_s, a2_r, a3_s, a3_r,
):
    r = lax.axis_index("row")
    c = lax.axis_index("col")
    core = lax.rem(r, 2)
    z = lax.rem(r // 2, NZ)
    xh = r // (2 * NZ)

    def rid(a, b, k):
        return (a * NZ + b) * 2 + k

    def zrel(o):
        return lax.rem(z + (o % NZ), NZ)

    def crel(o):
        return lax.rem(c + (o % NCOL), NCOL)

    def cid(yo, near):
        side = lax.rem(c, 2)
        return 2 * lax.rem(c // 2 + (yo % 4), 4) + (side if near == 0 else 1 - side)

    partner = (rid(xh, z, 1 - core), c)
    opposite = (rid(1 - xh, z, core), c)
    beside = (r, cid(0, 1))
    ypeer = [None] + [(r, cid(i, 0)) for i in range(1, 4)]
    far = (10, 11, 8, 9, 6, 7, 12, 13, 5, 4, 14, 15, 3, 2, 1)

    def flip(value, i):
        return value if i % 2 == 0 else 1 - value

    near_peer = [(rid(xh, z, flip(core, i)), crel(i // 2)) for i in range(16)]
    row_peer = [(rid(flip(xh, i), zrel(i // 2), core), c) for i in range(16)]
    zpeer = [None] + [(rid(xh, zrel(i), core), c) for i in range(1, NZ)]
    cpeer = [None] + [(r, crel(i)) for i in range(1, NCOL)]

    loads = [
        pltpu.make_async_copy(src, dst, load.at[i])
        for i, (src, dst) in enumerate(
            (
                (gout_hbm, gin),
                (feat_hbm, fbuf.at[pl.ds(2 * r, 2)]),
                (rows_hbm, rows),
                (cols_hbm, cols),
                (w_hbm, w),
            )
        )
    ]
    tile_copies = [
        pltpu.make_async_copy(
            tiles_hbm.at[pl.ds(64 * i, 64)], tv.at[pl.ds(64 * i, 64)], tile_sem.at[i]
        )
        for i in range(4)
    ]
    barrier = pltpu.get_barrier_semaphore()
    everyone = [zpeer[i] for i in (1, 2, 6, 7)] + ypeer[1:] + [beside, opposite, partner]
    for device in everyone:
        pl.semaphore_signal(
            barrier, inc=1, device_id=device, device_id_type=pl.DeviceIdType.MESH
        )
    for copy in loads:
        copy.start()
    for copy in tile_copies:
        copy.start()
    runs[EMPTY] = jnp.zeros((TB, F), jnp.float32)
    loads[0].wait()
    for blk in range(2):
        gbuf[2 * c + blk] = gin[blk].astype(jnp.float32).T.astype(jnp.bfloat16)
    loads[1].wait()
    pl.semaphore_wait(barrier, len(everyone))

    def col_shard(yo, near):
        return gbuf.at[pl.ds(2 * cid(yo, near), 2)]

    def col_copy(i, near, yo):
        here = col_shard(yo, near)
        return remote(here, here, col_s.at[near, i], col_r.at[near, i], ypeer[i])

    def side_copy(near):
        here = col_shard(0, near)
        return remote(here, here, col_s.at[0, 0], col_r.at[0, 0], beside)

    def shard(st, o, k):
        return fbuf.at[pl.ds(2 * rid(xh if st == 0 else 1 - xh, zrel(o), k), 2)]

    def z_copy(kind, way, o):
        sign = 1 if way == 0 else -1
        here = shard(1 if kind == NEXT_B else 0, o, core)
        if kind == FOURTH:
            here = fbuf.at[pl.ds(2 * rid(xh, zrel(o), core) + way, 1)]
        step = 2 if kind in (SECOND, FOURTH) else 1
        return remote(
            here, here, agz_s.at[kind, way], agz_r.at[kind, way], zpeer[(sign * step) % NZ]
        )

    def x_copy(o, st):
        here = shard(st, o, core)
        return remote(here, here, agx_s.at[o % NZ], agx_r.at[o % NZ], opposite)

    def p_copy(st, o, k):
        here = shard(st, o, k)
        return remote(here, here, agp_s.at[st, o % NZ], agp_r.at[st, o % NZ], partner)

    side_copy(0).start()
    for i in (2, 1, 3):
        col_copy(i, 0, 0).start()
    x_copy(0, 0).start()
    for way in range(2):
        z_copy(SECOND, way, 0).start()
    p_copy(0, 0, core).start()

    def arrive_z(kind, way):
        back = (1, 2, 3, 4, 1)[kind]
        o = -back if way == 0 else back
        z_copy(kind, way, o).wait_recv()
        if kind == SECOND:
            z_copy(THIRD, way, o).start()
            z_copy(FOURTH, way, o).start()
        if kind in (SECOND, THIRD):
            x_copy(o, 0).start()
        if kind == FOURTH:
            if way == 0:
                return
            x_copy(4, 0).start()
        p_copy(1 if kind == NEXT_B else 0, o, core).start()

    def arrive_x(o):
        x_copy(o, 1).wait_recv()
        p_copy(1, o, core).start()

    def arrive_side():
        side_copy(1).wait_recv()
        for i in (2, 1, 3):
            col_copy(i, 1, 0).start()

    loads[2].wait()
    loads[3].wait()
    live = count[0, 0]
    order, last = sorted_plan(cols[...], rows[...], live)
    plan_v[pl.ds(B_ORDER, 1)] = order
    plan_v[pl.ds(B_LAST, 1)] = last
    order, last = sorted_plan(rows[...], cols[...], live)
    plan_v[pl.ds(F_ORDER, 1)] = order
    plan_v[pl.ds(F_LAST, 1)] = last
    plan_copy = pltpu.make_async_copy(plan_v, plan, plan_sem.at[0])
    plan_copy.start()

    arrive_side()
    arrive_x(0)
    for way in range(2):
        arrive_z(SECOND, way)
    for way in range(2):
        z_copy(NEXT, way, 0).start()
        z_copy(NEXT_B, way, 0).start()

    plan_copy.wait()
    for copy in tile_copies:
        copy.wait()
    loads[4].wait()
    for near in range(2):
        for i in range(1, 4):
            col_copy(i, near, -i).wait_recv()

    def tile_step(which, i, acc, product):
        value = [plan[which, i * UNROLL + u] for u in range(UNROLL)]
        before = [plan[which, jnp.maximum(i * UNROLL - 1, 0)]] + value[:-1]
        terms = []
        for v in value:
            terms.append(product((v >> SLOT_BITS) & (SLOTS - 1), v))
        for u in range(UNROLL):
            same = (value[u] >> KEY_BITS) == (before[u] >> KEY_BITS)
            acc = acc * jnp.where(same, 1.0, 0.0) + terms[u]
            runs[i * UNROLL + u] = acc
        return acc

    def final_run(which, block):
        last = jnp.clip(plan[which, block], 0, EMPTY)
        return runs[last].astype(jnp.bfloat16)

    def backward(t, o):
        return jnp.dot(gbuf[o & (ROW_BLOCKS - 1)], tv[t], preferred_element_type=jnp.float32)

    def forward(t, o):
        return jnp.dot(tv[t], fbuf[o & (COL_BLOCKS - 1)], preferred_element_type=jnp.float32)

    def backward_body(i, acc):
        @pl.when(i == 0)
        def _():
            for way in range(2):
                arrive_z(THIRD, way)

        @pl.when(i == 2)
        def _():
            for way in range(2):
                arrive_z(FOURTH, way)

        @pl.when(i == 5)
        def _():
            arrive_x(2)
            arrive_x(6)

        return tile_step(B_ORDER, i, acc, backward)

    zero = jnp.zeros((TB, F), jnp.float32)
    lax.fori_loop(0, STEPS, backward_body, zero)

    def block_of(which, j, rel):
        k = 1 - core if which == 0 else core
        o = jnp.where(
            j == 0, 4, jnp.where(j == 7, 0, jnp.where(lax.rem(j, 2) == 1, 3 - j // 2, 4 + j // 2))
        )
        a = jnp.where(rel == 1, xh, 1 - xh)
        return 2 * rid(a, lax.rem(z + o, NZ), k)

    def extract(which, first, size):
        def body(j, carry):
            for rel in range(2):
                b = block_of(which, j, rel)
                for blk in range(2):
                    part[which, j, rel, blk] = final_run(B_LAST, b + blk)
            return carry

        lax.fori_loop(first, first + size, body, 0, unroll=True)

    def peer_copy(n):
        first, size = PIECES[n]
        return remote(
            part.at[0, pl.ds(first, size)], peer.at[pl.ds(first, size)],
            rp_s.at[n], rp_r.at[n], partner,
        )

    def rx_copy(o):
        return remote(x_out.at[o], x_in.at[o], rx_s.at[o], rx_r.at[o], opposite)

    def rz_copy(kind, way):
        sign = 1 if way == 0 else -1
        src, dst = z_out.at[kind, way], z_in.at[kind, way]
        if kind == FOURTH:
            src, dst = z_out.at[kind, way, way], z_in.at[kind, way, way]
        step = 2 if kind in (SECOND, FOURTH) else 1
        return remote(src, dst, rz_s.at[kind, way], rz_r.at[kind, way], zpeer[(sign * step) % NZ])

    def own(j, rel, blk):
        return part[1, j, rel, blk].astype(jnp.float32) + peer[j, rel, blk].astype(jnp.float32)

    for n, (first, size) in enumerate(PIECES):
        extract(0, first, size)
        peer_copy(n).start()
    extract(1, 0, NZ)
    place = {o: j for j, o in enumerate(OFFSETS)}

    def send_x(o):
        for blk in range(2):
            value = own(place[o], 0, blk)
            if o == 0:
                for way in range(2):
                    value = value + z_in[NEXT_B, way, blk].astype(jnp.float32)
            x_out[o, blk] = value.astype(jnp.bfloat16)
        rx_copy(o).start()

    def send_z(kind, way):
        o = (1, 2, 3, 4, 1)[kind] * (1 if way == 0 else -1) % NZ
        rel = 0 if kind == NEXT_B else 1
        if kind in (SECOND, THIRD) or (kind == FOURTH and way == 0):
            rx_copy(o).wait_recv()
        if kind == SECOND:
            for other in (THIRD, FOURTH):
                rz_copy(other, way).wait_recv()
        for blk in range(2):
            if kind == FOURTH and blk != way:
                continue
            value = own(place[o], rel, blk)
            if kind in (SECOND, THIRD, FOURTH):
                value = value + x_in[o, blk].astype(jnp.float32)
            if kind == SECOND:
                value = value + z_in[THIRD, way, blk].astype(jnp.float32)
                if blk == way:
                    value = value + z_in[FOURTH, way, blk].astype(jnp.float32)
            z_out[kind, way, blk] = value.astype(jnp.bfloat16)
        rz_copy(kind, way).start()

    for n in range(len(PIECES)):
        peer_copy(n).wait_recv()
        for o in ((4,), (3, 5), (2, 6), ())[n]:
            send_x(o)
    for kind in (NEXT_B, NEXT):
        for way in range(2):
            send_z(kind, way)

    for way in range(2):
        arrive_z(NEXT, way)
        arrive_z(NEXT_B, way)
    for o in (3, 5, 4):
        arrive_x(o)
    for st in range(2):
        for o in range(NZ):
            p_copy(st, o, 1 - core).wait_recv()

    def term_body(j, acc):
        for which in range(2):
            for rel in range(2):
                b = block_of(which, j, rel)
                left = jnp.concatenate([part[which, j, rel, 0], part[which, j, rel, 1]], axis=1)
                right = fbuf[pl.ds(b, 2)].reshape(2 * TB, F)
                acc = acc + jnp.dot(left, right, preferred_element_type=jnp.float32)
        return acc

    term = lax.fori_loop(0, NZ, term_body, zero, unroll=True)
    wt[...] = term.reshape(16, F // 16, F)

    def near_slot(i, sign):
        return crel(sign * (i // 2)) * 2 + flip(core, i)

    def row_slot(i):
        return flip(xh, i) * NZ + zrel(-(i // 2))

    def red1_copy(i):
        return remote(
            wt.at[near_slot(i, 1)], red1.at[i - 1], a1_s.at[i - 1], a1_r.at[i - 1], near_peer[i]
        )

    def red2_copy(i, owner):
        here = red2.at[owner]
        return remote(here, here, a2_s.at[i - 1], a2_r.at[i - 1], row_peer[i])

    def red3_copy(i, owner):
        here = red3.at[owner]
        return remote(here, here, a3_s.at[i - 1], a3_r.at[i - 1], near_peer[i])

    for i in far:
        red1_copy(i).start()

    def forward_body(i, acc):
        @pl.when(i == 4)
        def _():
            for way in range(2):
                send_z(FOURTH, way)

        @pl.when(i == 6)
        def _():
            for way in range(2):
                send_z(THIRD, way)

        return tile_step(F_ORDER, i, acc, forward)

    lax.fori_loop(0, STEPS, forward_body, zero)

    for i in range(1, 16):
        red1_copy(i).wait_recv()
    total = wt[near_slot(0, 1)]
    for i in range(15):
        total = total + red1[i]
    red2[row_slot(0)] = total
    for i in far:
        red2_copy(i, row_slot(0)).start()

    for way in range(2):
        rz_copy(NEXT_B, way).wait_recv()
    send_x(0)

    for b in range(ROW_BLOCKS):
        agg[b] = final_run(F_LAST, b)

    def agg_copy(i):
        return remote(
            agg.at[pl.ds(2 * crel(i), 2)], agg_in.at[i - 1], cr_s.at[i - 1], cr_r.at[i - 1], cpeer[i]
        )

    for i in (5, 3, 4, 6, 2, 7, 1):
        agg_copy(i).start()

    for way in range(2):
        send_z(SECOND, way)

    for i in range(1, 16):
        red2_copy(i, row_slot(i)).wait_recv()
    total = red2[0]
    for i in range(1, 16):
        total = total + red2[i]
    red3[near_slot(0, 1)] = total * (1.0 / math.sqrt(65536))
    for i in far:
        red3_copy(i, near_slot(0, 1)).start()


    for i in range(1, NCOL):
        agg_copy(i).wait_recv()
    for blk in range(2):
        total = agg[2 * c + blk].astype(jnp.float32)
        for i in range(NCOL - 1):
            total = total + agg_in[i, blk].astype(jnp.float32)
        lay_ref[blk] = jnp.dot(
            total.astype(jnp.bfloat16), w[...], preferred_element_type=jnp.float32
        ).astype(jnp.bfloat16)

    rx_copy(0).wait_recv()
    for kind in (NEXT, SECOND):
        for way in range(2):
            rz_copy(kind, way).wait_recv()
    for blk in range(2):
        total = own(place[0], 1, blk) + x_in[0, blk].astype(jnp.float32)
        for kind in (NEXT, SECOND):
            for way in range(2):
                total = total + z_in[kind, way, blk].astype(jnp.float32)
        upper = total.astype(jnp.bfloat16)
        lower = (total - upper.astype(jnp.float32)).astype(jnp.bfloat16)
        value = jnp.zeros((TB, F), jnp.float32)
        for share in (lower, upper):
            value = value + lax.dot_general(
                share, w[...], (((0,), (1,)), ((), ())), preferred_element_type=jnp.float32
            )
        gf_ref[blk] = value.astype(jnp.bfloat16)

    for i in range(1, 16):
        red3_copy(i, near_slot(i, -1)).wait_recv()
    gw_ref[...] = red3[...].reshape(F, F).T

    side_copy(0).wait_send()
    for i in range(1, NCOL):
        agg_copy(i).wait_send()
    for near in range(2):
        for i in range(1, 4):
            col_copy(i, near, 0).wait_send()
    for i in range(1, 16):
        red1_copy(i).wait_send()
        red2_copy(i, row_slot(0)).wait_send()
        red3_copy(i, near_slot(0, 1)).wait_send()
    for n in range(len(PIECES)):
        peer_copy(n).wait_send()
    for kind in range(5):
        for way in range(2):
            z_copy(kind, way, 0).wait_send()
            rz_copy(kind, way).wait_send()
    for o in (0, 2, 3, 4, 5, 6):
        x_copy(o, 0).wait_send()
        rx_copy(o).wait_send()
    for st in range(2):
        for o in range(NZ):
            p_copy(st, o, core).wait_send()


def hand_over(a, b, c, a_out, b_out, c_out, sem):
    copies = [
        pltpu.make_async_copy(src, dst, sem.at[i])
        for i, (src, dst) in enumerate(((a, a_out), (b, b_out), (c, c_out)))
    ]
    for copy in copies:
        copy.start()
    for copy in copies:
        copy.wait()


def per_device(features, tiles, tile_rows, tile_cols, tile_count, weight, grad_out):
    bf, f32, i32 = jnp.bfloat16, jnp.float32, jnp.int32
    dma = pltpu.SemaphoreType.DMA
    vmem = pl.BlockSpec(memory_space=pltpu.VMEM)
    hbm = pl.BlockSpec(memory_space=pltpu.HBM)
    pair = (2, TB, F)
    out_shape = (
        jax.ShapeDtypeStruct(pair, bf),
        jax.ShapeDtypeStruct(pair, bf),
        jax.ShapeDtypeStruct((F, F), f32),
    )
    made = pl.pallas_call(
        kernel,
        out_shape=out_shape,
        in_specs=[pl.BlockSpec(memory_space=pltpu.SMEM)] + [hbm] * 6,
        out_specs=(vmem, vmem, vmem),
        scratch_shapes=[
            pltpu.VMEM((1, SLOTS), i32),
            pltpu.VMEM((1, SLOTS), i32),
            pltpu.VMEM(pair, bf),
            pltpu.VMEM((F, F), bf),
            pltpu.VMEM((4, SLOTS), i32),
            pltpu.SMEM((4, SLOTS), i32),
            pltpu.VMEM((SLOTS, TB, TB), bf),
            pltpu.VMEM((COL_BLOCKS, TB, F), bf),
            pltpu.VMEM((ROW_BLOCKS, F, TB), bf),
            pltpu.VMEM((SLOTS + 1, TB, F), f32),
            pltpu.VMEM((2, NZ, 2, 2, F, TB), bf),
            pltpu.VMEM((NZ, 2, 2, F, TB), bf),
            pltpu.VMEM((NZ, 2, F, TB), bf),
            pltpu.VMEM((NZ, 2, F, TB), bf),
            pltpu.VMEM((5, 2, 2, F, TB), bf),
            pltpu.VMEM((5, 2, 2, F, TB), bf),
            pltpu.VMEM((ROW_BLOCKS, TB, F), bf),
            pltpu.VMEM((NCOL - 1, 2, TB, F), bf),
            pltpu.VMEM((16, F // 16, F), f32),
            pltpu.VMEM((15, F // 16, F), f32),
            pltpu.VMEM((16, F // 16, F), f32),
            pltpu.VMEM((16, F // 16, F), f32),
            dma((5,)), dma((4,)), dma((1,)), dma((2, 4)), dma((2, 4)), dma((5, 2)), dma((5, 2)),
            dma((NZ,)), dma((NZ,)), dma((2, NZ)), dma((2, NZ)),
            dma((4,)), dma((4,)), dma((NZ,)), dma((NZ,)), dma((5, 2)), dma((5, 2)), dma((7,)), dma((7,)),
            dma((15,)), dma((15,)), dma((15,)), dma((15,)), dma((15,)), dma((15,)),
        ],
        compiler_params=pltpu.CompilerParams(
            collective_id=0, has_side_effects=True, vmem_limit_bytes=63 * 2**20
        ),
        cost_estimate=pl.CostEstimate(
            flops=4 * SLOTS * TB * TB * F, bytes_accessed=2**23, transcendentals=0
        ),
        name="aggregate",
    )(
        tile_count,
        tile_rows.reshape(1, SLOTS),
        tile_cols.reshape(1, SLOTS),
        features.reshape(pair),
        grad_out.reshape(pair),
        weight,
        tiles.reshape(SLOTS, TB, TB),
    )
    lay, gf, gw = pl.pallas_call(
        hand_over,
        out_shape=out_shape,
        in_specs=[vmem] * 3,
        out_specs=(hbm,) * 3,
        scratch_shapes=[dma((3,))],
        name="hand_over",
    )(*made)
    return (lay.reshape(1, 2 * TB, F), gf.reshape(1, 2 * TB, F), gw)


def solution(mesh):
    in_specs = (
        P("col", "row", None),
        P("row", "col", None, None, None),
        P("row", "col", None),
        P("row", "col", None),
        P("row", "col"),
        P(),
        P("row", "col", None),
    )
    out_specs = (P("row", "col", None), P("col", "row", None), P())
    return jax.shard_map(
        per_device, mesh=mesh, in_specs=in_specs, out_specs=out_specs, check_vma=False
    )
```

```python
import math

import jax
import jax.numpy as jnp
from jax import lax
from jax.experimental import pallas as pl
from jax.experimental.pallas import tpu as pltpu
from jax.sharding import PartitionSpec as P

TB = 128
F = 128
SLOTS = 256
ROW_BLOCKS = 16
COL_BLOCKS = 64
NZ = 8
NCOL = 8
UNROLL = 32
STEPS = SLOTS // UNROLL
EMPTY = SLOTS
KEY_BITS = 16
SLOT_BITS = 8
OFFSETS = (4, 3, 5, 2, 6, 1, 7, 0)
PIECES = ((0, 1), (1, 2), (3, 2), (5, 3))
NEXT, SECOND, THIRD, FOURTH, NEXT_B = range(5)
B_ORDER, B_LAST, F_ORDER, F_LAST = range(4)


def remote(src, dst, send, recv, device):
    return pltpu.make_async_remote_copy(
        src_ref=src, dst_ref=dst, send_sem=send, recv_sem=recv,
        device_id=device, device_id_type=pl.DeviceIdType.MESH,
    )


def sorted_plan(key, other, count):
    lane = lax.broadcasted_iota(jnp.int32, (1, SLOTS), 1)
    key = jnp.where(lane < count, key, COL_BLOCKS)
    value = (key * 2**KEY_BITS + lane * 2**SLOT_BITS + other).astype(jnp.float32)
    across = lax.broadcasted_iota(jnp.int32, (SLOTS, SLOTS), 1)
    along = lax.broadcasted_iota(jnp.int32, (SLOTS, SLOTS), 0)
    column = jnp.sum(jnp.where(across == along, value, 0.0), axis=1, keepdims=True)
    place = jnp.sum(jnp.where(value < column, 1.0, 0.0), axis=1, keepdims=True)
    order = jnp.sum(jnp.where(place == across.astype(jnp.float32), column, 0.0), axis=0, keepdims=True)
    bound = (lane * 2**KEY_BITS).astype(jnp.float32)
    below = jnp.sum(jnp.where(column < bound, 1.0, 0.0), axis=0, keepdims=True)
    upto = jnp.sum(jnp.where(column < bound + 2.0**KEY_BITS, 1.0, 0.0), axis=0, keepdims=True)
    last = jnp.where(upto > below, upto - 1.0, float(EMPTY))
    return order.astype(jnp.int32), last.astype(jnp.int32)


def kernel(
    count, rows_hbm, cols_hbm, feat_hbm, gout_hbm, w_hbm, tiles_hbm, lay_ref, gf_ref, gw_ref,
    rows, cols, gin, w, plan_v, plan,
    tv, fbuf, gbuf, runs, part, peer, x_in, z_out, z_in,
    agg, agg_in, wt, red1, red2, red3,
    load, tile_sem, plan_sem, col_s, col_r, side_r, agz_s, agz_r, agx_s, agx_r, agp_s, agp_r,
    rp_s, rp_r, rx_s, rx_r, rz_s, rz_r, cr_s, cr_r,
    a1_s, a1_r, a2_s, a2_r, a3_s, a3_r,
):
    r = lax.axis_index("row")
    c = lax.axis_index("col")
    core = lax.rem(r, 2)
    z = lax.rem(r // 2, NZ)
    xh = r // (2 * NZ)

    def rid(a, b, k):
        return (a * NZ + b) * 2 + k

    def zrel(o):
        return lax.rem(z + (o % NZ), NZ)

    def crel(o):
        return lax.rem(c + (o % NCOL), NCOL)

    def cid(yo, near):
        side = lax.rem(c, 2)
        return 2 * lax.rem(c // 2 + (yo % 4), 4) + (side if near == 0 else 1 - side)

    partner = (rid(xh, z, 1 - core), c)
    opposite = (rid(1 - xh, z, core), c)
    beside = (r, cid(0, 1))
    ypeer = [None] + [(r, cid(i, 0)) for i in range(1, 4)]
    far = (10, 11, 8, 9, 6, 7, 12, 13, 5, 4, 14, 15, 3, 2, 1)

    def flip(value, i):
        return value if i % 2 == 0 else 1 - value

    near_peer = [(rid(xh, z, flip(core, i)), crel(i // 2)) for i in range(16)]
    row_peer = [(rid(flip(xh, i), zrel(i // 2), core), c) for i in range(16)]
    zpeer = [None] + [(rid(xh, zrel(i), core), c) for i in range(1, NZ)]
    cpeer = [None] + [(r, crel(i)) for i in range(1, NCOL)]

    def all_sent(like, sem):
        remote(like, like, sem.at[0], sem.at[0], partner).wait_send()

    def all_here(like, sem):
        remote(like, like, sem.at[0], sem.at[0], partner).wait_recv()

    loads = [
        pltpu.make_async_copy(src, dst, load.at[i])
        for i, (src, dst) in enumerate(
            (
                (gout_hbm, gin),
                (feat_hbm, fbuf.at[pl.ds(2 * r, 2)]),
                (rows_hbm, rows),
                (cols_hbm, cols),
                (w_hbm, w),
            )
        )
    ]
    tile_copy = pltpu.make_async_copy(tiles_hbm, tv, tile_sem.at[0])
    barrier = pltpu.get_barrier_semaphore()
    everyone = [zpeer[i] for i in (1, 2, 6, 7)] + ypeer[1:] + [beside, opposite, partner]
    for device in everyone:
        pl.semaphore_signal(
            barrier, inc=1, device_id=device, device_id_type=pl.DeviceIdType.MESH
        )
    for copy in loads:
        copy.start()
    tile_copy.start()
    runs[EMPTY] = jnp.zeros((TB, F), jnp.float32)
    loads[0].wait()
    for blk in range(2):
        gbuf[2 * c + blk] = gin[blk].astype(jnp.float32).T.astype(jnp.bfloat16)
    loads[1].wait()
    pl.semaphore_wait(barrier, len(everyone))

    def col_shard(yo, near):
        return gbuf.at[pl.ds(2 * cid(yo, near), 2)]

    def col_copy(i, near, yo):
        here = col_shard(yo, near)
        return remote(here, here, col_s.at[0], col_r.at[0], ypeer[i])

    def side_copy(near):
        here = col_shard(0, near)
        return remote(here, here, col_s.at[0], side_r.at[0], beside)

    def shard(st, o, k):
        return fbuf.at[pl.ds(2 * rid(xh if st == 0 else 1 - xh, zrel(o), k), 2)]

    def z_copy(kind, way, o):
        sign = 1 if way == 0 else -1
        here = shard(1 if kind == NEXT_B else 0, o, core)
        if kind == FOURTH:
            here = fbuf.at[pl.ds(2 * rid(xh, zrel(o), core) + way, 1)]
        step = 2 if kind in (SECOND, FOURTH) else 1
        return remote(
            here, here, agz_s.at[0], agz_r.at[kind, way], zpeer[(sign * step) % NZ]
        )

    def x_copy(o, st):
        here = shard(st, o, core)
        return remote(here, here, agx_s.at[0], agx_r.at[o % NZ], opposite)

    def p_copy(st, o, k):
        here = shard(st, o, k)
        return remote(here, here, agp_s.at[0], agp_r.at[0], partner)

    side_copy(0).start()
    for i in (2, 1, 3):
        col_copy(i, 0, 0).start()
    x_copy(0, 0).start()
    for way in range(2):
        z_copy(SECOND, way, 0).start()
    p_copy(0, 0, core).start()

    def arrive_z(kind, way):
        back = (1, 2, 3, 4, 1)[kind]
        o = -back if way == 0 else back
        z_copy(kind, way, o).wait_recv()
        if kind == SECOND:
            z_copy(THIRD, way, o).start()
            z_copy(FOURTH, way, o).start()
        if kind in (SECOND, THIRD):
            x_copy(o, 0).start()
        if kind == FOURTH:
            if way == 0:
                return
            x_copy(4, 0).start()
        p_copy(1 if kind == NEXT_B else 0, o, core).start()

    def arrive_x(o):
        x_copy(o, 1).wait_recv()
        p_copy(1, o, core).start()

    def arrive_side():
        side_copy(1).wait_recv()
        for i in (2, 1, 3):
            col_copy(i, 1, 0).start()

    loads[2].wait()
    loads[3].wait()
    live = count[0, 0]
    order, last = sorted_plan(cols[...], rows[...], live)
    plan_v[pl.ds(B_ORDER, 1)] = order
    plan_v[pl.ds(B_LAST, 1)] = last
    order, last = sorted_plan(rows[...], cols[...], live)
    plan_v[pl.ds(F_ORDER, 1)] = order
    plan_v[pl.ds(F_LAST, 1)] = last
    plan_copy = pltpu.make_async_copy(plan_v, plan, plan_sem.at[0])
    plan_copy.start()

    arrive_side()
    arrive_x(0)
    for way in range(2):
        arrive_z(SECOND, way)
    for way in range(2):
        z_copy(NEXT, way, 0).start()
        z_copy(NEXT_B, way, 0).start()

    plan_copy.wait()
    tile_copy.wait()
    loads[4].wait()
    all_here(gbuf.at[pl.ds(0, 12)], col_r)

    def tile_step(which, i, acc, product):
        value = [plan[which, i * UNROLL + u] for u in range(UNROLL)]
        before = [plan[which, jnp.maximum(i * UNROLL - 1, 0)]] + value[:-1]
        terms = []
        for v in value:
            terms.append(product((v >> SLOT_BITS) & (SLOTS - 1), v))
        for u in range(UNROLL):
            same = (value[u] >> KEY_BITS) == (before[u] >> KEY_BITS)
            acc = acc * jnp.where(same, 1.0, 0.0) + terms[u]
            runs[i * UNROLL + u] = acc
        return acc

    def final_run(which, block):
        last = jnp.clip(plan[which, block], 0, EMPTY)
        return runs[last].astype(jnp.bfloat16)

    def backward(t, o):
        return jnp.dot(gbuf[o & (ROW_BLOCKS - 1)], tv[t], preferred_element_type=jnp.float32)

    def forward(t, o):
        return jnp.dot(tv[t], fbuf[o & (COL_BLOCKS - 1)], preferred_element_type=jnp.float32)

    def backward_body(i, acc):
        @pl.when(i == 0)
        def _():
            for way in range(2):
                arrive_z(THIRD, way)

        @pl.when(i == 2)
        def _():
            for way in range(2):
                arrive_z(FOURTH, way)

        @pl.when(i == 5)
        def _():
            arrive_x(2)
            arrive_x(6)

        return tile_step(B_ORDER, i, acc, backward)

    zero = jnp.zeros((TB, F), jnp.float32)
    lax.fori_loop(0, STEPS, backward_body, zero)

    def block_of(which, j, rel):
        k = 1 - core if which == 0 else core
        o = jnp.where(
            j == 0, 4, jnp.where(j == 7, 0, jnp.where(lax.rem(j, 2) == 1, 3 - j // 2, 4 + j // 2))
        )
        a = jnp.where(rel == 1, xh, 1 - xh)
        return 2 * rid(a, lax.rem(z + o, NZ), k)

    place = {o: j for j, o in enumerate(OFFSETS)}

    def extract(which, first, size):
        def body(j, carry):
            for rel in range(2):
                b = block_of(which, j, rel)
                for blk in range(2):
                    part[which, j, rel, blk] = final_run(B_LAST, b + blk)
            return carry

        lax.fori_loop(first, first + size, body, 0, unroll=True)

    def peer_copy(n):
        first, size = PIECES[n]
        return remote(
            part.at[0, pl.ds(first, size)], peer.at[pl.ds(first, size)],
            rp_s.at[0], rp_r.at[n], partner,
        )

    def rx_copy(o):
        src = part.at[1, place[o], 0]
        return remote(src, x_in.at[o], rx_s.at[0], rx_r.at[o], opposite)

    def rz_copy(kind, way):
        sign = 1 if way == 0 else -1
        src, dst = z_out.at[kind, way], z_in.at[kind, way]
        if kind == FOURTH:
            src, dst = z_out.at[kind, way, way], z_in.at[kind, way, way]
        step = 2 if kind in (SECOND, FOURTH) else 1
        return remote(src, dst, rz_s.at[0], rz_r.at[kind, way], zpeer[(sign * step) % NZ])

    def own(j, rel, blk):
        return part[1, j, rel, blk].astype(jnp.float32)

    for n, (first, size) in enumerate(PIECES):
        extract(0, first, size)
        peer_copy(n).start()
    extract(1, 0, NZ)
    def pair_sum(j):
        for rel in range(2):
            for blk in range(2):
                value = own(j, rel, blk) + peer[j, rel, blk].astype(jnp.float32)
                part[1, j, rel, blk] = value.astype(jnp.bfloat16)

    def send_x0():
        for blk in range(2):
            value = own(place[0], 0, blk)
            for way in range(2):
                value = value + z_in[NEXT_B, way, blk].astype(jnp.float32)
            part[1, place[0], 0, blk] = value.astype(jnp.bfloat16)
        rx_copy(0).start()

    def send_z(kind, way):
        o = (1, 2, 3, 4, 1)[kind] * (1 if way == 0 else -1) % NZ
        rel = 0 if kind == NEXT_B else 1
        if kind in (SECOND, THIRD) or (kind == FOURTH and way == 0):
            rx_copy(o).wait_recv()
        if kind == SECOND:
            for other in (THIRD, FOURTH):
                rz_copy(other, way).wait_recv()
        for blk in range(2):
            if kind == FOURTH and blk != way:
                continue
            value = own(place[o], rel, blk)
            if kind in (SECOND, THIRD, FOURTH):
                value = value + x_in[o, blk].astype(jnp.float32)
            if kind == SECOND:
                value = value + z_in[THIRD, way, blk].astype(jnp.float32)
                if blk == way:
                    value = value + z_in[FOURTH, way, blk].astype(jnp.float32)
            z_out[kind, way, blk] = value.astype(jnp.bfloat16)
        rz_copy(kind, way).start()

    for n in range(len(PIECES)):
        peer_copy(n).wait_recv()
        first, size = PIECES[n]
        for j in range(first, first + size):
            pair_sum(j)
            if OFFSETS[j] in (2, 3, 4, 5, 6):
                rx_copy(OFFSETS[j]).start()
    for kind in (NEXT_B, NEXT):
        for way in range(2):
            send_z(kind, way)

    for way in range(2):
        arrive_z(NEXT, way)
        arrive_z(NEXT_B, way)
    for o in (3, 5, 4):
        arrive_x(o)
    def term_body(j, acc):
        for rel in range(2):
            b = block_of(1, j, rel)
            left = jnp.concatenate([part[1, j, rel, 0], part[1, j, rel, 1]], axis=1)
            right = fbuf[pl.ds(b, 2)].reshape(2 * TB, F)
            acc = acc + jnp.dot(left, right, preferred_element_type=jnp.float32)
        return acc

    term = lax.fori_loop(0, NZ, term_body, zero, unroll=True)
    wt[...] = term.reshape(16, F // 16, F)

    def near_slot(i, sign):
        return crel(sign * (i // 2)) * 2 + flip(core, i)

    def row_slot(i):
        return flip(xh, i) * NZ + zrel(-(i // 2))

    def red1_copy(i):
        return remote(
            wt.at[near_slot(i, 1)], red1.at[i - 1], a1_s.at[0], a1_r.at[0], near_peer[i]
        )

    def red2_copy(i, owner):
        here = red2.at[owner]
        return remote(here, here, a2_s.at[0], a2_r.at[0], row_peer[i])

    def red3_copy(i, owner):
        here = red3.at[owner]
        return remote(here, here, a3_s.at[0], a3_r.at[0], near_peer[i])

    for i in far:
        red1_copy(i).start()

    all_here(fbuf.at[pl.ds(0, 32)], agp_r)

    def forward_body(i, acc):
        @pl.when(i == 4)
        def _():
            for way in range(2):
                send_z(FOURTH, way)

        @pl.when(i == 6)
        def _():
            for way in range(2):
                send_z(THIRD, way)

        return tile_step(F_ORDER, i, acc, forward)

    lax.fori_loop(0, STEPS, forward_body, zero)

    all_here(red1, a1_r)
    total = wt[near_slot(0, 1)]
    for i in range(15):
        total = total + red1[i]
    red2[row_slot(0)] = total
    for i in far:
        red2_copy(i, row_slot(0)).start()

    for way in range(2):
        rz_copy(NEXT_B, way).wait_recv()
    send_x0()

    for b in range(ROW_BLOCKS):
        agg[b] = final_run(F_LAST, b)

    def agg_copy(i):
        return remote(
            agg.at[pl.ds(2 * crel(i), 2)], agg_in.at[i - 1], cr_s.at[0], cr_r.at[0], cpeer[i]
        )

    for i in (5, 3, 4, 6, 2, 7, 1):
        agg_copy(i).start()

    for way in range(2):
        send_z(SECOND, way)

    all_here(red2.at[pl.ds(0, 15)], a2_r)
    total = red2[0]
    for i in range(1, 16):
        total = total + red2[i]
    red3[near_slot(0, 1)] = total * (1.0 / math.sqrt(65536))
    for i in far:
        red3_copy(i, near_slot(0, 1)).start()


    all_here(agg_in, cr_r)
    for blk in range(2):
        total = agg[2 * c + blk].astype(jnp.float32)
        for i in range(NCOL - 1):
            total = total + agg_in[i, blk].astype(jnp.float32)
        lay_ref[blk] = jnp.dot(
            total.astype(jnp.bfloat16), w[...], preferred_element_type=jnp.float32
        ).astype(jnp.bfloat16)

    rx_copy(0).wait_recv()
    for kind in (NEXT, SECOND):
        for way in range(2):
            rz_copy(kind, way).wait_recv()
    for blk in range(2):
        total = own(place[0], 1, blk) + x_in[0, blk].astype(jnp.float32)
        for kind in (NEXT, SECOND):
            for way in range(2):
                total = total + z_in[kind, way, blk].astype(jnp.float32)
        upper = total.astype(jnp.bfloat16)
        lower = (total - upper.astype(jnp.float32)).astype(jnp.bfloat16)
        value = jnp.zeros((TB, F), jnp.float32)
        for share in (lower, upper):
            value = value + lax.dot_general(
                share, w[...], (((0,), (1,)), ((), ())), preferred_element_type=jnp.float32
            )
        gf_ref[blk] = value.astype(jnp.bfloat16)

    all_here(red3.at[pl.ds(0, 15)], a3_r)
    gw_ref[...] = red3[...].reshape(F, F).T

    for like, sem in (
        (gbuf.at[pl.ds(0, 14)], col_s),
        (fbuf.at[pl.ds(0, 18)], agz_s),
        (fbuf.at[pl.ds(0, 12)], agx_s),
        (fbuf.at[pl.ds(0, 32)], agp_s),
        (part.at[0], rp_s),
        (x_in.at[pl.ds(0, 6)], rx_s),
        (fbuf.at[pl.ds(0, 18)], rz_s),
        (agg_in, cr_s),
        (red1, a1_s),
        (red2.at[pl.ds(0, 15)], a2_s),
        (red3.at[pl.ds(0, 15)], a3_s),
    ):
        all_sent(like, sem)


def hand_over(a, b, c, a_out, b_out, c_out, sem):
    copies = [
        pltpu.make_async_copy(src, dst, sem.at[i])
        for i, (src, dst) in enumerate(((a, a_out), (b, b_out), (c, c_out)))
    ]
    for copy in copies:
        copy.start()
    for copy in copies:
        copy.wait()


def per_device(features, tiles, tile_rows, tile_cols, tile_count, weight, grad_out):
    bf, f32, i32 = jnp.bfloat16, jnp.float32, jnp.int32
    dma = pltpu.SemaphoreType.DMA
    vmem = pl.BlockSpec(memory_space=pltpu.VMEM)
    hbm = pl.BlockSpec(memory_space=pltpu.HBM)
    pair = (2, TB, F)
    out_shape = (
        jax.ShapeDtypeStruct(pair, bf),
        jax.ShapeDtypeStruct(pair, bf),
        jax.ShapeDtypeStruct((F, F), f32),
    )
    made = pl.pallas_call(
        kernel,
        out_shape=out_shape,
        in_specs=[pl.BlockSpec(memory_space=pltpu.SMEM)] + [hbm] * 6,
        out_specs=(vmem, vmem, vmem),
        scratch_shapes=[
            pltpu.VMEM((1, SLOTS), i32),
            pltpu.VMEM((1, SLOTS), i32),
            pltpu.VMEM(pair, bf),
            pltpu.VMEM((F, F), bf),
            pltpu.VMEM((4, SLOTS), i32),
            pltpu.SMEM((4, SLOTS), i32),
            pltpu.VMEM((SLOTS, TB, TB), bf),
            pltpu.VMEM((COL_BLOCKS, TB, F), bf),
            pltpu.VMEM((ROW_BLOCKS, F, TB), bf),
            pltpu.VMEM((SLOTS + 1, TB, F), f32),
            pltpu.VMEM((2, NZ, 2, 2, F, TB), bf),
            pltpu.VMEM((NZ, 2, 2, F, TB), bf),
            pltpu.VMEM((NZ, 2, F, TB), bf),
            pltpu.VMEM((5, 2, 2, F, TB), bf),
            pltpu.VMEM((5, 2, 2, F, TB), bf),
            pltpu.VMEM((ROW_BLOCKS, TB, F), bf),
            pltpu.VMEM((NCOL - 1, 2, TB, F), bf),
            pltpu.VMEM((16, F // 16, F), f32),
            pltpu.VMEM((15, F // 16, F), f32),
            pltpu.VMEM((16, F // 16, F), f32),
            pltpu.VMEM((16, F // 16, F), f32),
            dma((5,)), dma((1,)), dma((1,)), dma((1,)), dma((1,)), dma((1,)),
            dma((1,)), dma((5, 2)), dma((1,)), dma((NZ,)), dma((1,)), dma((1,)),
            dma((1,)), dma((4,)), dma((1,)), dma((NZ,)), dma((1,)), dma((5, 2)), dma((1,)), dma((1,)),
            dma((1,)), dma((1,)), dma((1,)), dma((1,)), dma((1,)), dma((1,)),
        ],
        compiler_params=pltpu.CompilerParams(
            collective_id=0, has_side_effects=True, vmem_limit_bytes=63 * 2**20
        ),
        cost_estimate=pl.CostEstimate(
            flops=4 * SLOTS * TB * TB * F, bytes_accessed=2**23, transcendentals=0
        ),
        name="aggregate",
    )(
        tile_count,
        tile_rows.reshape(1, SLOTS),
        tile_cols.reshape(1, SLOTS),
        features.reshape(pair),
        grad_out.reshape(pair),
        weight,
        tiles.reshape(SLOTS, TB, TB),
    )
    lay, gf, gw = pl.pallas_call(
        hand_over,
        out_shape=out_shape,
        in_specs=[vmem] * 3,
        out_specs=(hbm,) * 3,
        scratch_shapes=[dma((3,))],
        name="hand_over",
    )(*made)
    return (lay.reshape(1, 2 * TB, F), gf.reshape(1, 2 * TB, F), gw)


def solution(mesh):
    in_specs = (
        P("col", "row", None),
        P("row", "col", None, None, None),
        P("row", "col", None),
        P("row", "col", None),
        P("row", "col"),
        P(),
        P("row", "col", None),
    )
    out_specs = (P("row", "col", None), P("col", "row", None), P())
    return jax.shard_map(
        per_device, mesh=mesh, in_specs=in_specs, out_specs=out_specs, check_vma=False
    )
```

```python
import math

import jax
import jax.numpy as jnp
from jax import lax
from jax.experimental import pallas as pl
from jax.experimental.pallas import tpu as pltpu
from jax.sharding import PartitionSpec as P

TB = 128
F = 128
SLOTS = 256
ROW_BLOCKS = 16
COL_BLOCKS = 64
NZ = 8
NCOL = 8
UNROLL = 32
STEPS = SLOTS // UNROLL
EMPTY = SLOTS
KEY_BITS = 16
SLOT_BITS = 8
OFFSETS = (4, 3, 5, 2, 6, 1, 7, 0)
PIECES = ((0, 1), (1, 2), (3, 2), (5, 3))
NEXT, SECOND, THIRD, FOURTH, NEXT_B = range(5)
B_ORDER, B_LAST, F_ORDER, F_LAST = range(4)


def remote(src, dst, send, recv, device):
    return pltpu.make_async_remote_copy(
        src_ref=src, dst_ref=dst, send_sem=send, recv_sem=recv,
        device_id=device, device_id_type=pl.DeviceIdType.MESH,
    )


def sorted_plan(key, other, count):
    lane = lax.broadcasted_iota(jnp.int32, (1, SLOTS), 1)
    key = jnp.where(lane < count, key, COL_BLOCKS)
    value = (key * 2**KEY_BITS + lane * 2**SLOT_BITS + other).astype(jnp.float32)
    across = lax.broadcasted_iota(jnp.int32, (SLOTS, SLOTS), 1)
    along = lax.broadcasted_iota(jnp.int32, (SLOTS, SLOTS), 0)
    column = jnp.sum(jnp.where(across == along, value, 0.0), axis=1, keepdims=True)
    place = jnp.sum(jnp.where(value < column, 1.0, 0.0), axis=1, keepdims=True)
    order = jnp.sum(jnp.where(place == across.astype(jnp.float32), column, 0.0), axis=0, keepdims=True)
    bound = (lane * 2**KEY_BITS).astype(jnp.float32)
    below = jnp.sum(jnp.where(column < bound, 1.0, 0.0), axis=0, keepdims=True)
    upto = jnp.sum(jnp.where(column < bound + 2.0**KEY_BITS, 1.0, 0.0), axis=0, keepdims=True)
    last = jnp.where(upto > below, upto - 1.0, float(EMPTY))
    return order.astype(jnp.int32), last.astype(jnp.int32)


def kernel(
    count, rows_hbm, cols_hbm, feat_hbm, gout_hbm, w_hbm, tiles_hbm, lay_ref, gf_ref, gw_ref,
    rows, cols, gin, w, plan_v, plan,
    tv, fbuf, gbuf, runs, part, peer, x_in, z_out, z_in,
    agg, agg_in, wt, red1, red2, red3,
    load, tile_sem, plan_sem, col_s, col_r, side_r, agz_s, agz_r, agx_s, agx_r, agp_s, agp_r,
    rp_s, rp_r, rx_s, rx_r, rz_s, rz_r, cr_s, cr_r,
    a1_s, a1_r, a2_s, a2_r, a3_s, a3_r,
):
    r = lax.axis_index("row")
    c = lax.axis_index("col")
    core = lax.rem(r, 2)
    z = lax.rem(r // 2, NZ)
    xh = r // (2 * NZ)

    def rid(a, b, k):
        return (a * NZ + b) * 2 + k

    def zrel(o):
        return lax.rem(z + (o % NZ), NZ)

    def crel(o):
        return lax.rem(c + (o % NCOL), NCOL)

    def cid(yo, near):
        side = lax.rem(c, 2)
        return 2 * lax.rem(c // 2 + (yo % 4), 4) + (side if near == 0 else 1 - side)

    partner = (rid(xh, z, 1 - core), c)
    opposite = (rid(1 - xh, z, core), c)
    beside = (r, cid(0, 1))
    ypeer = [None] + [(r, cid(i, 0)) for i in range(1, 4)]
    far = (10, 11, 8, 9, 6, 7, 12, 13, 5, 4, 14, 15, 3, 2, 1)

    def flip(value, i):
        return value if i % 2 == 0 else 1 - value

    near_peer = [(rid(xh, z, flip(core, i)), crel(i // 2)) for i in range(16)]
    row_peer = [(rid(flip(xh, i), zrel(i // 2), core), c) for i in range(16)]
    zpeer = [None] + [(rid(xh, zrel(i), core), c) for i in range(1, NZ)]
    cpeer = [None] + [(r, crel(i)) for i in range(1, NCOL)]

    def all_sent(like, sem):
        remote(like, like, sem.at[0], sem.at[0], partner).wait_send()

    def all_here(like, sem):
        remote(like, like, sem.at[0], sem.at[0], partner).wait_recv()

    loads = [
        pltpu.make_async_copy(src, dst, load.at[i])
        for i, (src, dst) in enumerate(
            (
                (gout_hbm, gin),
                (feat_hbm, fbuf.at[pl.ds(2 * r, 2)]),
                (rows_hbm, rows),
                (cols_hbm, cols),
                (w_hbm, w),
            )
        )
    ]
    tile_copy = pltpu.make_async_copy(tiles_hbm, tv, tile_sem.at[0])
    barrier = pltpu.get_barrier_semaphore()
    everyone = [zpeer[i] for i in (1, 2, 6, 7)] + ypeer[1:] + [beside, opposite, partner]
    for device in everyone:
        pl.semaphore_signal(
            barrier, inc=1, device_id=device, device_id_type=pl.DeviceIdType.MESH
        )
    for copy in loads:
        copy.start()
    tile_copy.start()
    runs[EMPTY] = jnp.zeros((TB, F), jnp.float32)
    loads[0].wait()
    for blk in range(2):
        gbuf[2 * c + blk] = gin[blk].astype(jnp.float32).T.astype(jnp.bfloat16)
    loads[1].wait()
    pl.semaphore_wait(barrier, len(everyone))

    def col_shard(yo, near):
        return gbuf.at[pl.ds(2 * cid(yo, near), 2)]

    def col_copy(i, near, yo):
        here = col_shard(yo, near)
        return remote(here, here, col_s.at[0], col_r.at[0], ypeer[i])

    def side_copy(near):
        here = col_shard(0, near)
        return remote(here, here, col_s.at[0], side_r.at[0], beside)

    def shard(st, o, k):
        return fbuf.at[pl.ds(2 * rid(xh if st == 0 else 1 - xh, zrel(o), k), 2)]

    def z_copy(kind, way, o):
        sign = 1 if way == 0 else -1
        here = shard(1 if kind == NEXT_B else 0, o, core)
        if kind == FOURTH:
            here = fbuf.at[pl.ds(2 * rid(xh, zrel(o), core) + way, 1)]
        step = 2 if kind in (SECOND, FOURTH) else 1
        return remote(
            here, here, agz_s.at[0], agz_r.at[kind, way], zpeer[(sign * step) % NZ]
        )

    def x_copy(o, st):
        here = shard(st, o, core)
        return remote(here, here, agx_s.at[0], agx_r.at[o % NZ], opposite)

    def p_copy(st, o, k):
        here = shard(st, o, k)
        return remote(here, here, agp_s.at[0], agp_r.at[0], partner)

    side_copy(0).start()
    for i in (2, 1, 3):
        col_copy(i, 0, 0).start()
    x_copy(0, 0).start()
    for way in range(2):
        z_copy(SECOND, way, 0).start()
    p_copy(0, 0, core).start()

    def arrive_z(kind, way):
        back = (1, 2, 3, 4, 1)[kind]
        o = -back if way == 0 else back
        z_copy(kind, way, o).wait_recv()
        if kind == SECOND:
            z_copy(THIRD, way, o).start()
            z_copy(FOURTH, way, o).start()
        if kind in (SECOND, THIRD):
            x_copy(o, 0).start()
        if kind == FOURTH:
            if way == 0:
                return
            x_copy(4, 0).start()
        p_copy(1 if kind == NEXT_B else 0, o, core).start()

    def arrive_x(o):
        x_copy(o, 1).wait_recv()
        p_copy(1, o, core).start()

    def arrive_side():
        side_copy(1).wait_recv()
        for i in (2, 1, 3):
            col_copy(i, 1, 0).start()

    loads[2].wait()
    loads[3].wait()
    live = count[0, 0]
    order, last = sorted_plan(cols[...], rows[...], live)
    plan_v[pl.ds(B_ORDER, 1)] = order
    plan_v[pl.ds(B_LAST, 1)] = last
    order, last = sorted_plan(rows[...], cols[...], live)
    plan_v[pl.ds(F_ORDER, 1)] = order
    plan_v[pl.ds(F_LAST, 1)] = last
    plan_copy = pltpu.make_async_copy(plan_v, plan, plan_sem.at[0])
    plan_copy.start()

    arrive_side()
    arrive_x(0)
    for way in range(2):
        arrive_z(SECOND, way)
    for way in range(2):
        z_copy(NEXT, way, 0).start()
        z_copy(NEXT_B, way, 0).start()

    plan_copy.wait()
    tile_copy.wait()
    loads[4].wait()
    all_here(gbuf.at[pl.ds(0, 12)], col_r)

    def tile_step(which, i, acc, product):
        value = [plan[which, i * UNROLL + u] for u in range(UNROLL)]
        before = [plan[which, jnp.maximum(i * UNROLL - 1, 0)]] + value[:-1]
        terms = []
        for v in value:
            terms.append(product((v >> SLOT_BITS) & (SLOTS - 1), v))
        for u in range(UNROLL):
            same = (value[u] >> KEY_BITS) == (before[u] >> KEY_BITS)
            acc = acc * jnp.where(same, 1.0, 0.0) + terms[u]
            runs[i * UNROLL + u] = acc
        return acc

    def final_run(which, block):
        last = jnp.clip(plan[which, block], 0, EMPTY)
        return runs[last].astype(jnp.bfloat16)

    def backward(t, o):
        return jnp.dot(gbuf[o & (ROW_BLOCKS - 1)], tv[t], preferred_element_type=jnp.float32)

    def forward(t, o):
        return jnp.dot(tv[t], fbuf[o & (COL_BLOCKS - 1)], preferred_element_type=jnp.float32)

    def backward_body(i, acc):
        @pl.when(i == 4)
        def _():
            for way in range(2):
                arrive_z(THIRD, way)

        @pl.when(i == 6)
        def _():
            for way in range(2):
                arrive_z(FOURTH, way)

        @pl.when(i == 7)
        def _():
            arrive_x(2)
            arrive_x(6)

        return tile_step(B_ORDER, i, acc, backward)

    zero = jnp.zeros((TB, F), jnp.float32)
    lax.fori_loop(0, STEPS, backward_body, zero)

    def block_of(which, j, rel):
        k = 1 - core if which == 0 else core
        o = jnp.where(
            j == 0, 4, jnp.where(j == 7, 0, jnp.where(lax.rem(j, 2) == 1, 3 - j // 2, 4 + j // 2))
        )
        a = jnp.where(rel == 1, xh, 1 - xh)
        return 2 * rid(a, lax.rem(z + o, NZ), k)

    place = {o: j for j, o in enumerate(OFFSETS)}

    def extract(which, first, size):
        def body(j, carry):
            for rel in range(2):
                b = block_of(which, j, rel)
                for blk in range(2):
                    part[which, j, rel, blk] = final_run(B_LAST, b + blk)
            return carry

        lax.fori_loop(first, first + size, body, 0, unroll=True)

    def peer_copy(n):
        first, size = PIECES[n]
        return remote(
            part.at[0, pl.ds(first, size)], peer.at[pl.ds(first, size)],
            rp_s.at[0], rp_r.at[n], partner,
        )

    def rx_copy(o):
        src = part.at[1, place[o], 0]
        return remote(src, x_in.at[o], rx_s.at[0], rx_r.at[o], opposite)

    def rz_copy(kind, way):
        sign = 1 if way == 0 else -1
        src, dst = z_out.at[kind, way], z_in.at[kind, way]
        if kind == FOURTH:
            src, dst = z_out.at[kind, way, way], z_in.at[kind, way, way]
        step = 2 if kind in (SECOND, FOURTH) else 1
        return remote(src, dst, rz_s.at[0], rz_r.at[kind, way], zpeer[(sign * step) % NZ])

    def own(j, rel, blk):
        return part[1, j, rel, blk].astype(jnp.float32)

    for n, (first, size) in enumerate(PIECES):
        extract(0, first, size)
        peer_copy(n).start()
    extract(1, 0, NZ)
    def pair_sum(j):
        for rel in range(2):
            for blk in range(2):
                value = own(j, rel, blk) + peer[j, rel, blk].astype(jnp.float32)
                part[1, j, rel, blk] = value.astype(jnp.bfloat16)

    def send_x0():
        for blk in range(2):
            value = own(place[0], 0, blk)
            for way in range(2):
                value = value + z_in[NEXT_B, way, blk].astype(jnp.float32)
            part[1, place[0], 0, blk] = value.astype(jnp.bfloat16)
        rx_copy(0).start()

    def send_z(kind, way):
        o = (1, 2, 3, 4, 1)[kind] * (1 if way == 0 else -1) % NZ
        rel = 0 if kind == NEXT_B else 1
        if kind in (SECOND, THIRD) or (kind == FOURTH and way == 0):
            rx_copy(o).wait_recv()
        if kind == SECOND:
            for other in (THIRD, FOURTH):
                rz_copy(other, way).wait_recv()
        for blk in range(2):
            if kind == FOURTH and blk != way:
                continue
            value = own(place[o], rel, blk)
            if kind in (SECOND, THIRD, FOURTH):
                value = value + x_in[o, blk].astype(jnp.float32)
            if kind == SECOND:
                value = value + z_in[THIRD, way, blk].astype(jnp.float32)
                if blk == way:
                    value = value + z_in[FOURTH, way, blk].astype(jnp.float32)
            z_out[kind, way, blk] = value.astype(jnp.bfloat16)
        rz_copy(kind, way).start()

    for n in range(len(PIECES)):
        peer_copy(n).wait_recv()
        first, size = PIECES[n]
        for j in range(first, first + size):
            pair_sum(j)
            if OFFSETS[j] in (2, 3, 4, 5, 6):
                rx_copy(OFFSETS[j]).start()
    for kind in (NEXT_B, NEXT):
        for way in range(2):
            send_z(kind, way)

    for way in range(2):
        arrive_z(NEXT, way)
        arrive_z(NEXT_B, way)
    for o in (3, 5, 4):
        arrive_x(o)
    def term_body(j, acc):
        for rel in range(2):
            b = block_of(1, j, rel)
            left = jnp.concatenate([part[1, j, rel, 0], part[1, j, rel, 1]], axis=1)
            right = fbuf[pl.ds(b, 2)].reshape(2 * TB, F)
            acc = acc + jnp.dot(left, right, preferred_element_type=jnp.float32)
        return acc

    term = lax.fori_loop(0, NZ, term_body, zero, unroll=True)
    wt[...] = term.reshape(16, F // 16, F)

    def near_slot(i, sign):
        return crel(sign * (i // 2)) * 2 + flip(core, i)

    def row_slot(i):
        return flip(xh, i) * NZ + zrel(-(i // 2))

    def red1_copy(i):
        return remote(
            wt.at[near_slot(i, 1)], red1.at[i - 1], a1_s.at[0], a1_r.at[0], near_peer[i]
        )

    def red2_copy(i, owner):
        here = red2.at[owner]
        return remote(here, here, a2_s.at[0], a2_r.at[0], row_peer[i])

    def red3_copy(i, owner):
        here = red3.at[owner]
        return remote(here, here, a3_s.at[0], a3_r.at[0], near_peer[i])

    for i in far:
        red1_copy(i).start()

    all_here(fbuf.at[pl.ds(0, 32)], agp_r)

    def forward_body(i, acc):
        @pl.when(i == 4)
        def _():
            for way in range(2):
                send_z(FOURTH, way)

        @pl.when(i == 6)
        def _():
            for way in range(2):
                send_z(THIRD, way)

        return tile_step(F_ORDER, i, acc, forward)

    lax.fori_loop(0, STEPS, forward_body, zero)

    all_here(red1, a1_r)
    total = wt[near_slot(0, 1)]
    for i in range(15):
        total = total + red1[i]
    red2[row_slot(0)] = total
    for i in far:
        red2_copy(i, row_slot(0)).start()

    for way in range(2):
        rz_copy(NEXT_B, way).wait_recv()
    send_x0()

    for b in range(ROW_BLOCKS):
        agg[b] = final_run(F_LAST, b)

    def agg_copy(i):
        return remote(
            agg.at[pl.ds(2 * crel(i), 2)], agg_in.at[i - 1], cr_s.at[0], cr_r.at[0], cpeer[i]
        )

    for i in (5, 3, 4, 6, 2, 7, 1):
        agg_copy(i).start()

    for way in range(2):
        send_z(SECOND, way)

    all_here(red2.at[pl.ds(0, 15)], a2_r)
    total = red2[0]
    for i in range(1, 16):
        total = total + red2[i]
    red3[near_slot(0, 1)] = total * (1.0 / math.sqrt(65536))
    for i in far:
        red3_copy(i, near_slot(0, 1)).start()


    all_here(agg_in, cr_r)
    for blk in range(2):
        total = agg[2 * c + blk].astype(jnp.float32)
        for i in range(NCOL - 1):
            total = total + agg_in[i, blk].astype(jnp.float32)
        lay_ref[blk] = jnp.dot(
            total.astype(jnp.bfloat16), w[...], preferred_element_type=jnp.float32
        ).astype(jnp.bfloat16)

    rx_copy(0).wait_recv()
    for kind in (NEXT, SECOND):
        for way in range(2):
            rz_copy(kind, way).wait_recv()
    for blk in range(2):
        total = own(place[0], 1, blk) + x_in[0, blk].astype(jnp.float32)
        for kind in (NEXT, SECOND):
            for way in range(2):
                total = total + z_in[kind, way, blk].astype(jnp.float32)
        upper = total.astype(jnp.bfloat16)
        lower = (total - upper.astype(jnp.float32)).astype(jnp.bfloat16)
        value = jnp.zeros((TB, F), jnp.float32)
        for share in (lower, upper):
            value = value + lax.dot_general(
                share, w[...], (((0,), (1,)), ((), ())), preferred_element_type=jnp.float32
            )
        gf_ref[blk] = value.astype(jnp.bfloat16)

    all_here(red3.at[pl.ds(0, 15)], a3_r)
    gw_ref[...] = red3[...].reshape(F, F).T

    for like, sem in (
        (gbuf.at[pl.ds(0, 14)], col_s),
        (fbuf.at[pl.ds(0, 18)], agz_s),
        (fbuf.at[pl.ds(0, 12)], agx_s),
        (fbuf.at[pl.ds(0, 32)], agp_s),
        (part.at[0], rp_s),
        (x_in.at[pl.ds(0, 6)], rx_s),
        (fbuf.at[pl.ds(0, 18)], rz_s),
        (agg_in, cr_s),
        (red1, a1_s),
        (red2.at[pl.ds(0, 15)], a2_s),
        (red3.at[pl.ds(0, 15)], a3_s),
    ):
        all_sent(like, sem)


def hand_over(a, b, c, a_out, b_out, c_out, sem):
    copies = [
        pltpu.make_async_copy(src, dst, sem.at[i])
        for i, (src, dst) in enumerate(((a, a_out), (b, b_out), (c, c_out)))
    ]
    for copy in copies:
        copy.start()
    for copy in copies:
        copy.wait()


def per_device(features, tiles, tile_rows, tile_cols, tile_count, weight, grad_out):
    bf, f32, i32 = jnp.bfloat16, jnp.float32, jnp.int32
    dma = pltpu.SemaphoreType.DMA
    vmem = pl.BlockSpec(memory_space=pltpu.VMEM)
    hbm = pl.BlockSpec(memory_space=pltpu.HBM)
    pair = (2, TB, F)
    out_shape = (
        jax.ShapeDtypeStruct(pair, bf),
        jax.ShapeDtypeStruct(pair, bf),
        jax.ShapeDtypeStruct((F, F), f32),
    )
    made = pl.pallas_call(
        kernel,
        out_shape=out_shape,
        in_specs=[pl.BlockSpec(memory_space=pltpu.SMEM)] + [hbm] * 6,
        out_specs=(vmem, vmem, vmem),
        scratch_shapes=[
            pltpu.VMEM((1, SLOTS), i32),
            pltpu.VMEM((1, SLOTS), i32),
            pltpu.VMEM(pair, bf),
            pltpu.VMEM((F, F), bf),
            pltpu.VMEM((4, SLOTS), i32),
            pltpu.SMEM((4, SLOTS), i32),
            pltpu.VMEM((SLOTS, TB, TB), bf),
            pltpu.VMEM((COL_BLOCKS, TB, F), bf),
            pltpu.VMEM((ROW_BLOCKS, F, TB), bf),
            pltpu.VMEM((SLOTS + 1, TB, F), f32),
            pltpu.VMEM((2, NZ, 2, 2, F, TB), bf),
            pltpu.VMEM((NZ, 2, 2, F, TB), bf),
            pltpu.VMEM((NZ, 2, F, TB), bf),
            pltpu.VMEM((5, 2, 2, F, TB), bf),
            pltpu.VMEM((5, 2, 2, F, TB), bf),
            pltpu.VMEM((ROW_BLOCKS, TB, F), bf),
            pltpu.VMEM((NCOL - 1, 2, TB, F), bf),
            pltpu.VMEM((16, F // 16, F), f32),
            pltpu.VMEM((15, F // 16, F), f32),
            pltpu.VMEM((16, F // 16, F), f32),
            pltpu.VMEM((16, F // 16, F), f32),
            dma((5,)), dma((1,)), dma((1,)), dma((1,)), dma((1,)), dma((1,)),
            dma((1,)), dma((5, 2)), dma((1,)), dma((NZ,)), dma((1,)), dma((1,)),
            dma((1,)), dma((4,)), dma((1,)), dma((NZ,)), dma((1,)), dma((5, 2)), dma((1,)), dma((1,)),
            dma((1,)), dma((1,)), dma((1,)), dma((1,)), dma((1,)), dma((1,)),
        ],
        compiler_params=pltpu.CompilerParams(
            collective_id=0, has_side_effects=True, vmem_limit_bytes=63 * 2**20
        ),
        cost_estimate=pl.CostEstimate(
            flops=4 * SLOTS * TB * TB * F, bytes_accessed=2**23, transcendentals=0
        ),
        name="aggregate",
    )(
        tile_count,
        tile_rows.reshape(1, SLOTS),
        tile_cols.reshape(1, SLOTS),
        features.reshape(pair),
        grad_out.reshape(pair),
        weight,
        tiles.reshape(SLOTS, TB, TB),
    )
    lay, gf, gw = pl.pallas_call(
        hand_over,
        out_shape=out_shape,
        in_specs=[vmem] * 3,
        out_specs=(hbm,) * 3,
        scratch_shapes=[dma((3,))],
        name="hand_over",
    )(*made)
    return (lay.reshape(1, 2 * TB, F), gf.reshape(1, 2 * TB, F), gw)


def solution(mesh):
    in_specs = (
        P("col", "row", None),
        P("row", "col", None, None, None),
        P("row", "col", None),
        P("row", "col", None),
        P("row", "col"),
        P(),
        P("row", "col", None),
    )
    out_specs = (P("row", "col", None), P("col", "row", None), P())
    return jax.shard_map(
        per_device, mesh=mesh, in_specs=in_specs, out_specs=out_specs, check_vma=False
    )
```
